256 devices in a mesh: rot: 4 (over z_hi), tx: 16 (over x, y), ty: 4 (over z_lo, core).
Axes of the slice: x: 4, y: 4, z: 8 (z_hi: 4, z_lo: 2; z = z_hi * 2 + z_lo), core: 2. Of those that a mesh axis runs over, the one named last changes fastest.
Arguments:
- tomogram: float32 [512, 128, 64], P('tx', 'ty'), may hold values from -60 to 60
- templates: float32 [8, 32, 1024], P('rot'), may hold values from -6 to 6
Outputs:
- top_score: float32 [512, 4096], P('tx', 'ty')
- next_score: float32 [512, 4096], P('tx', 'ty')
The draws below stay inside these ranges and needn't reach their ends.
All inputs are finite; a program needn't handle non-finite values.
Results may differ from the reference program's by a relative error of at most 0.0003.
Values sent between devices are 32-bit elements; how exact they have to be, the bound alone decides.
No kernel may reach another device: no remote copies, remote signals or barrier semaphores. Data moves between devices by JAX's collectives and lax.ppermute only.
A program may use at most 128 MiB of HBM per device.

```python
import math
import jax
import jax.numpy as jnp
from jax import lax

TEMPLATE = 32
HALO = 16
RADIUS = 15
ZD = 32
ZE = 64
NX = 512
NY = 128
ROTS = 8


def draw_tomogram(key, part):
    key = jax.random.fold_in(key, 11)
    noise_key, scale_key = jax.random.split(key, 2)
    levels = jax.random.uniform(scale_key, (NX // 4, NY // 4, ZE // 4), jnp.float32, 0.0, math.log(10.0))
    scales = jnp.exp(levels)
    scales = jnp.repeat(jnp.repeat(jnp.repeat(scales, 4, axis=0), 4, axis=1), 4, axis=2)
    noise = jnp.clip(jax.random.normal(noise_key, (NX, NY, ZE), jnp.float32), -6.0, 6.0)
    return noise * scales


def level_of(stream_key, shape, cuts, smallest, largest):
    def one(dim, blocks):
        heights = jax.random.uniform(jax.random.fold_in(jax.random.fold_in(stream_key, 6), dim), (blocks,), jnp.float32, smallest / len(cuts), largest / len(cuts))
        return jnp.repeat(jnp.exp(heights), shape[dim] // blocks).reshape((-1,) + (1,) * (len(shape) - dim - 1))

    gain = one(*cuts[0])
    for cut in cuts[1:]:
        gain = gain * one(*cut)
    return gain


def bell_draw(stream_key, dims, deviation, reach, pieces=(), held_as=jnp.bfloat16):
    drawn = jax.random.normal(stream_key, dims, jnp.float32) * deviation
    if len(pieces) > 0:
        drawn = level_of(stream_key, dims, pieces, -0.22, 0.18) * drawn
    return jnp.clip(drawn, min=-reach, max=reach).astype(held_as)


def setup_inputs(seed: int = 0) -> dict:
    key_of = jax.random.split(jax.random.key(seed), 3)
    tomogram = draw_tomogram(jax.random.fold_in(key_of[2], 71), 0)
    templates = bell_draw(key_of[1], (ROTS, TEMPLATE, TEMPLATE * TEMPLATE), 1.0, 6.0, ((0, 4),), jnp.float32)
    return {"tomogram": tomogram, "templates": templates}


epsilon = 1e-05

def sphere(box_edge):
    centred = jnp.arange(box_edge, dtype=jnp.float32) - (box_edge - 1) / 2.0
    radius_sq = centred[:, None, None] ** 2 + centred[None, :, None] ** 2 + centred[None, None, :] ** 2
    return (radius_sq <= float(RADIUS * RADIUS)).astype(jnp.float32)

def reference(tomogram, templates):
    padded = jnp.pad(tomogram, ((HALO, HALO), (HALO, HALO), (0, 0)))
    grid_shape = padded.shape
    spectrum = jnp.fft.rfftn(padded)
    square_spec = jnp.fft.rfftn(padded * padded)
    sphere_mask = sphere(TEMPLATE)
    filled = jnp.sum(sphere_mask)

    def correlate(spec_in, kernel):
        kernel_spec = jnp.fft.rfftn(kernel, s=grid_shape)
        circular = jnp.fft.irfftn(spec_in * jnp.conj(kernel_spec), s=grid_shape)
        return circular[:NX, :NY, :ZD].astype(jnp.float32)
    local_sum = correlate(spectrum, sphere_mask)
    local_sq = correlate(square_spec, sphere_mask)
    local_std = jnp.sqrt(local_sq / filled - (local_sum / filled) ** 2 + epsilon)
    divisor = jnp.sqrt(filled) * local_std
    shaped = templates.reshape(ROTS, TEMPLATE, TEMPLATE, TEMPLATE)

    def advance(carry, template):
        top_score, next_score = carry
        masked_mean = jnp.sum(template * sphere_mask) / filled
        spread = jnp.sum(sphere_mask * (template - masked_mean) ** 2) / filled
        normed = sphere_mask * (template - masked_mean) / jnp.sqrt(spread + epsilon)
        rot_score = correlate(spectrum, normed) / divisor
        next_score = jnp.maximum(next_score, jnp.minimum(top_score, rot_score))
        top_score = jnp.maximum(top_score, rot_score)
        return ((top_score, next_score), None)
    start = jnp.full((NX, NY, ZD), -1e+30, jnp.float32)
    (top_score, next_score), _ = lax.scan(advance, (start, start), shaped)
    return (top_score.reshape(NX, NY * ZD), next_score.reshape(NX, NY * ZD))
```

```python
import functools

import jax
import jax.numpy as jnp
import ml_dtypes
import numpy as np
from jax import lax
from jax.experimental import pallas as pl
from jax.experimental.pallas import tpu as pltpu
from jax.sharding import PartitionSpec as P

RADIUS = 15
EPSILON = 1e-05
GRID = 64
BOX = 32
HALF = 16
LANES = 128
SETS = 4
F32 = jnp.float32
BF16 = jnp.bfloat16


def halves(table):
    hi = table.astype(ml_dtypes.bfloat16)
    lo = (table - hi.astype(np.float64)).astype(ml_dtypes.bfloat16)
    return hi, lo


def wave(out_pos, in_pos):
    angle = 2.0 * np.pi / GRID * np.outer(out_pos, in_pos)
    return np.cos(angle), np.sin(angle)


def left_table(blocks):
    parts = []
    for block in blocks:
        hi, lo = halves(block)
        parts += [hi, hi, lo]
    return np.concatenate(parts, axis=1)


def sphere_np():
    centred = np.arange(BOX) - (BOX - 1) / 2.0
    sq = centred[:, None, None] ** 2 + centred[None, :, None] ** 2 + centred[None, None, :] ** 2
    return (sq <= float(RADIUS * RADIUS)).astype(np.float64)


@functools.cache
def tables():
    freq = np.arange(GRID)
    cos_f, sin_f = wave(freq, np.arange(GRID))
    forward = left_table([np.concatenate([cos_f, sin_f], axis=0)])
    cos_t, sin_t = wave(freq, np.arange(BOX))
    kernel = left_table([cos_t, sin_t])

    def inverse(shift):
        cos_i, sin_i = wave(np.arange(BOX) + shift, freq)
        return left_table([np.concatenate([cos_i, sin_i], axis=0) / GRID])

    cz, sz = cos_f.T, sin_f.T
    zero = np.zeros((GRID, LANES))
    plain = np.concatenate([cz, -sz], axis=1)
    turned = np.concatenate([sz, cz], axis=1)
    tomo_z = np.block([[plain, zero, plain, zero], [zero, plain, zero, plain], [zero, zero, turned, zero], [zero, zero, zero, turned]])
    ct, st = cos_t.T, sin_t.T
    one = np.concatenate([ct, st], axis=1)
    two = np.concatenate([-st, ct], axis=1)
    kern_z = np.concatenate([np.kron(np.eye(4), one), np.kron(np.eye(4), two)], axis=0)

    def inverse_z(shift):
        cos_i, sin_i = wave(freq, np.arange(BOX) + shift)
        real = np.concatenate([cos_i, -sin_i], axis=0) / GRID
        imag = np.concatenate([sin_i, cos_i], axis=0) / GRID
        return np.concatenate([np.kron(np.eye(4), real), np.kron(np.eye(4), imag)], axis=1)

    centre = (BOX - 1) / 2.0
    sphere = sphere_np()
    cos_m, _ = wave(freq, np.arange(BOX) - centre)
    sin_m = wave(freq, np.arange(BOX) - centre)[1]
    spec = sphere.astype(np.complex128)
    for axis in range(3):
        spec = np.moveaxis(np.tensordot(cos_m + 1j * sin_m, spec, axes=(1, axis)), 0, axis)
    real = np.transpose(spec.real, (1, 0, 2))
    mask_spec = np.concatenate([real, real], axis=2).astype(np.float32)
    mask = sphere.reshape(BOX, BOX * BOX).astype(np.float32)
    return (
        mask,
        mask_spec,
        *halves(tomo_z),
        *halves(kern_z),
        forward,
        kernel,
        inverse(0.0),
        inverse(centre),
        *halves(inverse_z(0.0)),
        *halves(inverse_z(centre)),
    )


def split(x):
    hi = x.astype(BF16)
    return hi, (x - hi.astype(F32)).astype(BF16)


def dot(a, b):
    return jnp.dot(a, b, preferred_element_type=F32)


def swapped(x):
    return pltpu.roll(x, GRID, 1)


def column(x):
    hi, lo = split(x)
    return jnp.concatenate([hi, lo, hi], axis=0)


def right_dot(x, w_hi, w_lo):
    hi, lo = split(x)
    return dot(hi, w_hi) + dot(lo, w_hi) + dot(hi, w_lo)


def body(
    own_ref, before_ref, after_ref, t_own_ref, t_far_ref, t_core_ref,
    mask_ref, mask_spec_ref, tz_hi, tz_lo, kz_hi, kz_lo, fwd_ref, ker_ref, inv_ref, inv_m_ref,
    iz_hi, iz_lo, im_hi, im_lo,
    top_ref, next_ref,
    fz, fy, kz, ky, vx, vy,
):
    filled = float(sphere_np().sum())
    lane = lax.broadcasted_iota(jnp.int32, (1, LANES), 1)
    plus_first = jnp.where(lane < GRID, 1.0, -1.0).astype(F32)
    first = lane < GRID

    mask = mask_ref[...]

    def normed(t):
        mu = jnp.sum(jnp.sum(t * mask, axis=0, keepdims=True), axis=1, keepdims=True) / filled
        d = (t - mu) * mask
        v = jnp.sum(jnp.sum(d * d, axis=0, keepdims=True), axis=1, keepdims=True) / filled
        return d / jnp.sqrt(v + EPSILON)

    pairs = [(t_own_ref[0], t_own_ref[1])] + [(t_far_ref[s], t_core_ref[s]) for s in range(3)]
    for p in range(SETS):
        a, b = normed(pairs[p][0]), normed(pairs[p][1])
        rows = [
            jnp.concatenate([a[:, LANES * g : LANES * (g + 1)], b[:, LANES * g : LANES * (g + 1)]], axis=1)
            for g in range(8)
        ]
        out = right_dot(jnp.concatenate(rows, axis=0), kz_hi[...], kz_lo[...])
        for g in range(8):
            for jj in range(4):
                j = 4 * g + jj
                kz[p, BOX * j : BOX * (j + 1), :] = out[BOX * g : BOX * (g + 1), LANES * jj : LANES * (jj + 1)]

    def two(x):
        return jnp.concatenate([column(x), column(swapped(x) * -plus_first)], axis=0)

    @pl.loop(0, BOX, step=2)
    def _(i):
        for p in range(SETS):
            rhs = [two(kz[p, pl.ds(i + e, BOX, stride=BOX), :]) for e in range(2)]
            out = dot(ker_ref[...], jnp.concatenate(rhs, axis=1))
            for e in range(2):
                ky[p, pl.ds(pl.multiple_of((i + e) * GRID, GRID), GRID), :] = out[:, LANES * e : LANES * (e + 1)]

    @pl.loop(0, BOX, step=4)
    def _(x):
        mid = own_ref[pl.ds(x, 4)].reshape(4 * BOX, LANES)
        low = before_ref[pl.ds(x, 4)].reshape(4 * HALF, LANES)
        high = after_ref[pl.ds(x, 4)].reshape(4 * HALF, LANES)
        rows = jnp.concatenate([mid, low, high], axis=0)
        out = right_dot(jnp.concatenate([rows, rows * rows], axis=1), tz_hi[...], tz_lo[...])
        for c in range(4):
            col = out[:, LANES * c : LANES * (c + 1)]
            for e in range(4):
                base = pl.multiple_of((x + e + BOX * (c % 2)) * GRID, GRID)
                fz[c // 2, pl.ds(base + HALF, BOX), :] = col[BOX * e : BOX * (e + 1)]
                fz[c // 2, pl.ds(base, HALF), :] = col[128 + HALF * e : 128 + HALF * (e + 1)]
                fz[c // 2, pl.ds(base + HALF + BOX, HALF), :] = col[192 + HALF * e : 192 + HALF * (e + 1)]

    def forward(a, b):
        out = dot(fwd_ref[...], jnp.concatenate([column(a), column(b)], axis=1))
        res = []
        for e in range(2):
            o = out[:, LANES * e : LANES * (e + 1)]
            res.append(o[:GRID] + swapped(o[GRID:]) * plus_first)
        return res

    def inverse(a, b, table):
        out = dot(table, jnp.concatenate([column(a), column(b)], axis=1))
        res = []
        for e in range(2):
            o = out[:, LANES * e : LANES * (e + 1)]
            res.append(o[:BOX] - swapped(o[BOX:]) * plus_first)
        return res

    @pl.loop(0, GRID, step=2)
    def _(x):
        for c in range(2):
            at = [pl.ds(pl.multiple_of((x + e) * GRID, GRID), GRID) for e in range(2)]
            res = forward(fz[c, at[0], :], fz[c, at[1], :])
            for e in range(2):
                fy[c, at[e], :] = res[e]

    @pl.loop(0, GRID, step=2)
    def _(k):
        spec = forward(*[fy[0, pl.ds(k + e, GRID, stride=GRID), :] for e in range(2)])
        same, cross = [], []
        for s in spec:
            r = swapped(s)
            same.append(jnp.where(first, s, r))
            cross.append(jnp.where(first, -r, s))
        for p in range(SETS):
            rhs = [two(ky[p, pl.ds(k + e, BOX, stride=GRID), :]) for e in range(2)]
            t = dot(ker_ref[...], jnp.concatenate(rhs, axis=1))
            prod = []
            for e in range(2):
                te = t[:, LANES * e : LANES * (e + 1)]
                prod.append(te * same[e] + swapped(te) * cross[e])
            res = inverse(prod[0], prod[1], inv_ref[...])
            for e in range(2):
                vx[p, pl.ds(pl.multiple_of((k + e) * BOX, BOX), BOX), :] = res[e]
        both = forward(*[fy[1, pl.ds(k + e, GRID, stride=GRID), :] for e in range(2)])
        res = inverse(both[0] * mask_spec_ref[k], both[1] * mask_spec_ref[k + 1], inv_m_ref[...])
        for e in range(2):
            vx[SETS, pl.ds(pl.multiple_of((k + e) * BOX, BOX), BOX), :] = res[e]

    @pl.loop(0, BOX, step=2)
    def _(x):
        for p in range(SETS + 1):
            cols = [vx[p, pl.ds(x + e, GRID, stride=BOX), :] for e in range(2)]
            res = inverse(cols[0], cols[1], inv_ref[...] if p < SETS else inv_m_ref[...])
            for e in range(2):
                vy[p, pl.ds(pl.multiple_of((x + e) * BOX, BOX), BOX), :] = res[e]

    def last(p, w_hi, w_lo):
        rows = []
        for g in range(8):
            rows.append(
                jnp.concatenate([vy[p, pl.ds(4 * g + yy, BOX, stride=BOX), :] for yy in range(4)], axis=1)
            )
        out = right_dot(jnp.concatenate(rows, axis=0), w_hi, w_lo)
        return out[:, :LANES], out[:, LANES:]

    total, square = last(SETS, im_hi[...], im_lo[...])
    mean = total / filled
    var = jnp.maximum(square / filled - mean * mean, 0.0)
    scale = 1.0 / (np.float32(np.sqrt(filled)) * jnp.sqrt(var + EPSILON))
    top, second = None, None
    for p in range(SETS):
        one, other = last(p, iz_hi[...], iz_lo[...])
        one, other = one * scale, other * scale
        high, low = jnp.maximum(one, other), jnp.minimum(one, other)
        if top is None:
            top, second = high, low
        else:
            second = jnp.maximum(jnp.minimum(top, high), jnp.maximum(second, low))
            top = jnp.maximum(top, high)
    for g in range(8):
        top_ref[:, LANES * g : LANES * (g + 1)] = top[BOX * g : BOX * (g + 1)]
        next_ref[:, LANES * g : LANES * (g + 1)] = second[BOX * g : BOX * (g + 1)]


def shifts(count, step):
    return [(i, i + step) for i in range(count) if 0 <= i + step < count]


def local(tomogram, templates):
    tx, ty, rots = lax.axis_size("tx"), lax.axis_size("ty"), lax.axis_size("rot")

    def pack(part):
        return jnp.concatenate([part[:, :HALF], part[:, HALF:]], axis=2)

    def unpack(part):
        return jnp.concatenate([part[:, :, :GRID], part[:, :, GRID:]], axis=1)

    before = lax.ppermute(pack(tomogram[HALF:]), "tx", shifts(tx, 1))
    after = lax.ppermute(pack(tomogram[:HALF]), "tx", shifts(tx, -1))

    core = lax.rem(lax.axis_index("ty"), 2)
    mine = lax.dynamic_slice_in_dim(templates, core, 1, axis=0)
    far = [lax.ppermute(mine, "rot", [(i, (i + s) % rots) for i in range(rots)]) for s in range(1, rots)]
    far = jnp.concatenate(far, axis=0)
    core_far = lax.ppermute(far, "ty", [(i, i + 1 - 2 * (i % 2)) for i in range(ty)])

    grid = jnp.concatenate(
        [
            jnp.concatenate([unpack(before), tomogram[:HALF]], axis=0),
            jnp.concatenate([tomogram[HALF:], unpack(after)], axis=0),
        ],
        axis=2,
    )
    low = lax.ppermute(grid[:, HALF:], "ty", shifts(ty, 1))
    high = lax.ppermute(grid[:, :HALF], "ty", shifts(ty, -1))

    out = jax.ShapeDtypeStruct((BOX, BOX * BOX), F32)
    scratch = [
        pltpu.VMEM((2, GRID * GRID, LANES), F32),
        pltpu.VMEM((2, GRID * GRID, LANES), F32),
        pltpu.VMEM((SETS, BOX * BOX, LANES), F32),
        pltpu.VMEM((SETS, BOX * GRID, LANES), F32),
        pltpu.VMEM((SETS + 1, BOX * GRID, LANES), F32),
        pltpu.VMEM((SETS + 1, BOX * BOX, LANES), F32),
    ]
    return pl.pallas_call(
        body,
        out_shape=(out, out),
        scratch_shapes=scratch,
        compiler_params=pltpu.CompilerParams(vmem_limit_bytes=56 * 1024 * 1024),
        cost_estimate=pl.CostEstimate(flops=10**10, bytes_accessed=10**7, transcendentals=0),
        name="scores",
    )(grid, low, high, templates, far, core_far, *[jnp.asarray(t) for t in tables()])


def solution(mesh):
    placed = (P("tx", "ty", None), P("rot", None, None))
    return jax.shard_map(
        local, mesh=mesh, in_specs=placed, out_specs=(P("tx", "ty"), P("tx", "ty")), check_vma=False
    )
```

```python
import functools

import jax
import jax.numpy as jnp
import ml_dtypes
import numpy as np
from jax import lax
from jax.experimental import pallas as pl
from jax.experimental.pallas import tpu as pltpu
from jax.sharding import PartitionSpec as P

RADIUS = 15
EPSILON = 1e-05
GRID = 64
BOX = 32
HALF = 16
LANES = 128
SETS = 4
F32 = jnp.float32
BF16 = jnp.bfloat16


def halves(table):
    hi = table.astype(ml_dtypes.bfloat16)
    lo = (table - hi.astype(np.float64)).astype(ml_dtypes.bfloat16)
    return hi, lo


def wave(out_pos, in_pos):
    angle = 2.0 * np.pi / GRID * np.outer(out_pos, in_pos)
    return np.cos(angle), np.sin(angle)


def left_table(blocks):
    parts = []
    for block in blocks:
        hi, lo = halves(block)
        parts += [hi, hi, lo]
    return np.concatenate(parts, axis=1)


def sphere_np():
    centred = np.arange(BOX) - (BOX - 1) / 2.0
    sq = centred[:, None, None] ** 2 + centred[None, :, None] ** 2 + centred[None, None, :] ** 2
    return (sq <= float(RADIUS * RADIUS)).astype(np.float64)


@functools.cache
def tables():
    freq = np.arange(GRID)
    cos_f, sin_f = wave(freq, np.arange(GRID))
    forward = left_table([np.concatenate([cos_f, sin_f], axis=0)])
    cos_t, sin_t = wave(freq, np.arange(BOX))
    kernel = left_table([cos_t, sin_t])

    def inverse(shift):
        cos_i, sin_i = wave(np.arange(BOX) + shift, freq)
        return left_table([np.concatenate([cos_i, sin_i], axis=0) / GRID])

    cz, sz = cos_f.T, sin_f.T
    zero = np.zeros((GRID, LANES))
    plain = np.concatenate([cz, -sz], axis=1)
    turned = np.concatenate([sz, cz], axis=1)
    tomo_z = np.block([[plain, zero, plain, zero], [zero, plain, zero, plain], [zero, zero, turned, zero], [zero, zero, zero, turned]])
    ct, st = cos_t.T, sin_t.T
    one = np.concatenate([ct, st], axis=1)
    two = np.concatenate([-st, ct], axis=1)
    kern_z = np.concatenate([np.kron(np.eye(4), one), np.kron(np.eye(4), two)], axis=0)

    def inverse_z(shift):
        cos_i, sin_i = wave(freq, np.arange(BOX) + shift)
        real = np.concatenate([cos_i, -sin_i], axis=0) / GRID
        imag = np.concatenate([sin_i, cos_i], axis=0) / GRID
        return np.concatenate([np.kron(np.eye(4), real), np.kron(np.eye(4), imag)], axis=1)

    centre = (BOX - 1) / 2.0
    sphere = sphere_np()
    cos_m, _ = wave(freq, np.arange(BOX) - centre)
    sin_m = wave(freq, np.arange(BOX) - centre)[1]
    spec = sphere.astype(np.complex128)
    for axis in range(3):
        spec = np.moveaxis(np.tensordot(cos_m + 1j * sin_m, spec, axes=(1, axis)), 0, axis)
    real = np.transpose(spec.real, (1, 0, 2))
    mask_spec = np.concatenate([real, real], axis=2).astype(np.float32)
    mask = sphere.reshape(BOX, BOX * BOX).astype(np.float32)
    return (
        mask,
        mask_spec,
        *halves(tomo_z),
        *halves(kern_z),
        forward,
        kernel,
        inverse(0.0),
        inverse(centre),
        *halves(inverse_z(0.0)),
        *halves(inverse_z(centre)),
    )


def split(x):
    hi = x.astype(BF16)
    return hi, (x - hi.astype(F32)).astype(BF16)


def dot(a, b):
    return jnp.dot(a, b, preferred_element_type=F32)


def swapped(x):
    return pltpu.roll(x, GRID, 1)


def column(x):
    hi, lo = split(x)
    return jnp.concatenate([hi, lo, hi], axis=0)


def right_dot(x, w_hi, w_lo):
    hi, lo = split(x)
    return dot(hi, w_hi) + dot(lo, w_hi) + dot(hi, w_lo)


def body(
    own_ref, before_ref, after_ref, t_own_ref, t_far_ref, t_core_ref,
    mask_ref, mask_spec_ref, tz_hi, tz_lo, kz_hi, kz_lo, fwd_ref, ker_ref, inv_ref, inv_m_ref,
    iz_hi, iz_lo, im_hi, im_lo,
    top_ref, next_ref,
    fz, fy, kz, ky, vx, vy,
):
    filled = float(sphere_np().sum())
    lane = lax.broadcasted_iota(jnp.int32, (1, LANES), 1)
    plus_first = jnp.where(lane < GRID, 1.0, -1.0).astype(F32)
    first = lane < GRID

    mask = mask_ref[...]

    def normed(t):
        mu = jnp.sum(jnp.sum(t * mask, axis=0, keepdims=True), axis=1, keepdims=True) / filled
        d = (t - mu) * mask
        v = jnp.sum(jnp.sum(d * d, axis=0, keepdims=True), axis=1, keepdims=True) / filled
        return d / jnp.sqrt(v + EPSILON)

    pairs = [(t_own_ref[0], t_own_ref[1])] + [(t_far_ref[s], t_core_ref[s]) for s in range(3)]
    for p in range(SETS):
        a, b = normed(pairs[p][0]), normed(pairs[p][1])
        rows = [
            jnp.concatenate([a[:, LANES * g : LANES * (g + 1)], b[:, LANES * g : LANES * (g + 1)]], axis=1)
            for g in range(8)
        ]
        out = right_dot(jnp.concatenate(rows, axis=0), kz_hi[...], kz_lo[...])
        for g in range(8):
            for jj in range(4):
                j = 4 * g + jj
                kz[p, BOX * j : BOX * (j + 1), :] = out[BOX * g : BOX * (g + 1), LANES * jj : LANES * (jj + 1)]

    def two(x):
        return jnp.concatenate([column(x), column(swapped(x) * -plus_first)], axis=0)

    @pl.loop(0, BOX, step=2, unroll=8)
    def _(i):
        for p in range(SETS):
            rhs = [two(kz[p, pl.ds(i + e, BOX, stride=BOX), :]) for e in range(2)]
            out = dot(ker_ref[...], jnp.concatenate(rhs, axis=1))
            for e in range(2):
                ky[p, pl.ds(pl.multiple_of((i + e) * GRID, GRID), GRID), :] = out[:, LANES * e : LANES * (e + 1)]

    @pl.loop(0, BOX, step=4)
    def _(x):
        mid = own_ref[pl.ds(x, 4)].reshape(4 * BOX, LANES)
        low = before_ref[pl.ds(x, 4)].reshape(4 * HALF, LANES)
        high = after_ref[pl.ds(x, 4)].reshape(4 * HALF, LANES)
        rows = jnp.concatenate([mid, low, high], axis=0)
        out = right_dot(jnp.concatenate([rows, rows * rows], axis=1), tz_hi[...], tz_lo[...])
        for c in range(4):
            col = out[:, LANES * c : LANES * (c + 1)]
            for e in range(4):
                base = pl.multiple_of((x + e + BOX * (c % 2)) * GRID, GRID)
                fz[c // 2, pl.ds(base + HALF, BOX), :] = col[BOX * e : BOX * (e + 1)]
                fz[c // 2, pl.ds(base, HALF), :] = col[128 + HALF * e : 128 + HALF * (e + 1)]
                fz[c // 2, pl.ds(base + HALF + BOX, HALF), :] = col[192 + HALF * e : 192 + HALF * (e + 1)]

    def forward(a, b):
        out = dot(fwd_ref[...], jnp.concatenate([column(a), column(b)], axis=1))
        res = []
        for e in range(2):
            o = out[:, LANES * e : LANES * (e + 1)]
            res.append(o[:GRID] + swapped(o[GRID:]) * plus_first)
        return res

    def inverse(a, b, table):
        out = dot(table, jnp.concatenate([column(a), column(b)], axis=1))
        res = []
        for e in range(2):
            o = out[:, LANES * e : LANES * (e + 1)]
            res.append(o[:BOX] - swapped(o[BOX:]) * plus_first)
        return res

    @pl.loop(0, GRID, step=2, unroll=8)
    def _(x):
        for c in range(2):
            at = [pl.ds(pl.multiple_of((x + e) * GRID, GRID), GRID) for e in range(2)]
            res = forward(fz[c, at[0], :], fz[c, at[1], :])
            for e in range(2):
                fy[c, at[e], :] = res[e]

    @pl.loop(0, GRID, step=2, unroll=8)
    def _(k):
        spec = forward(*[fy[0, pl.ds(k + e, GRID, stride=GRID), :] for e in range(2)])
        same, cross = [], []
        for s in spec:
            r = swapped(s)
            same.append(jnp.where(first, s, r))
            cross.append(jnp.where(first, -r, s))
        for p in range(SETS):
            rhs = [two(ky[p, pl.ds(k + e, BOX, stride=GRID), :]) for e in range(2)]
            t = dot(ker_ref[...], jnp.concatenate(rhs, axis=1))
            prod = []
            for e in range(2):
                te = t[:, LANES * e : LANES * (e + 1)]
                prod.append(te * same[e] + swapped(te) * cross[e])
            res = inverse(prod[0], prod[1], inv_ref[...])
            for e in range(2):
                vx[p, pl.ds(pl.multiple_of((k + e) * BOX, BOX), BOX), :] = res[e]
        both = forward(*[fy[1, pl.ds(k + e, GRID, stride=GRID), :] for e in range(2)])
        res = inverse(both[0] * mask_spec_ref[k], both[1] * mask_spec_ref[k + 1], inv_m_ref[...])
        for e in range(2):
            vx[SETS, pl.ds(pl.multiple_of((k + e) * BOX, BOX), BOX), :] = res[e]

    @pl.loop(0, BOX, step=2, unroll=8)
    def _(x):
        for p in range(SETS + 1):
            cols = [vx[p, pl.ds(x + e, GRID, stride=BOX), :] for e in range(2)]
            res = inverse(cols[0], cols[1], inv_ref[...] if p < SETS else inv_m_ref[...])
            for e in range(2):
                vy[p, pl.ds(pl.multiple_of((x + e) * BOX, BOX), BOX), :] = res[e]

    def last(p, w_hi, w_lo):
        rows = []
        for g in range(8):
            rows.append(
                jnp.concatenate([vy[p, pl.ds(4 * g + yy, BOX, stride=BOX), :] for yy in range(4)], axis=1)
            )
        out = right_dot(jnp.concatenate(rows, axis=0), w_hi, w_lo)
        return out[:, :LANES], out[:, LANES:]

    total, square = last(SETS, im_hi[...], im_lo[...])
    mean = total / filled
    var = jnp.maximum(square / filled - mean * mean, 0.0)
    scale = 1.0 / (np.float32(np.sqrt(filled)) * jnp.sqrt(var + EPSILON))
    top, second = None, None
    for p in range(SETS):
        one, other = last(p, iz_hi[...], iz_lo[...])
        one, other = one * scale, other * scale
        high, low = jnp.maximum(one, other), jnp.minimum(one, other)
        if top is None:
            top, second = high, low
        else:
            second = jnp.maximum(jnp.minimum(top, high), jnp.maximum(second, low))
            top = jnp.maximum(top, high)
    for g in range(8):
        top_ref[:, LANES * g : LANES * (g + 1)] = top[BOX * g : BOX * (g + 1)]
        next_ref[:, LANES * g : LANES * (g + 1)] = second[BOX * g : BOX * (g + 1)]


def shifts(count, step):
    return [(i, i + step) for i in range(count) if 0 <= i + step < count]


def local(tomogram, templates):
    tx, ty, rots = lax.axis_size("tx"), lax.axis_size("ty"), lax.axis_size("rot")

    def pack(part):
        return jnp.concatenate([part[:, :HALF], part[:, HALF:]], axis=2)

    def unpack(part):
        return jnp.concatenate([part[:, :, :GRID], part[:, :, GRID:]], axis=1)

    before = lax.ppermute(pack(tomogram[HALF:]), "tx", shifts(tx, 1))
    after = lax.ppermute(pack(tomogram[:HALF]), "tx", shifts(tx, -1))

    core = lax.rem(lax.axis_index("ty"), 2)
    mine = lax.dynamic_slice_in_dim(templates, core, 1, axis=0)
    far = [lax.ppermute(mine, "rot", [(i, (i + s) % rots) for i in range(rots)]) for s in range(1, rots)]
    far = jnp.concatenate(far, axis=0)
    core_far = lax.ppermute(far, "ty", [(i, i + 1 - 2 * (i % 2)) for i in range(ty)])

    grid = jnp.concatenate(
        [
            jnp.concatenate([unpack(before), tomogram[:HALF]], axis=0),
            jnp.concatenate([tomogram[HALF:], unpack(after)], axis=0),
        ],
        axis=2,
    )
    low = lax.ppermute(grid[:, HALF:], "ty", shifts(ty, 1))
    high = lax.ppermute(grid[:, :HALF], "ty", shifts(ty, -1))

    return kernel_call(grid, low, high, templates, far, core_far)


def kernel_call(grid, low, high, templates, far, core_far):
    out = jax.ShapeDtypeStruct((BOX, BOX * BOX), F32)
    scratch = [
        pltpu.VMEM((2, GRID * GRID, LANES), F32),
        pltpu.VMEM((2, GRID * GRID, LANES), F32),
        pltpu.VMEM((SETS, BOX * BOX, LANES), F32),
        pltpu.VMEM((SETS, BOX * GRID, LANES), F32),
        pltpu.VMEM((SETS + 1, BOX * GRID, LANES), F32),
        pltpu.VMEM((SETS + 1, BOX * BOX, LANES), F32),
    ]
    return pl.pallas_call(
        body,
        out_shape=(out, out),
        scratch_shapes=scratch,
        compiler_params=pltpu.CompilerParams(vmem_limit_bytes=56 * 1024 * 1024),
        cost_estimate=pl.CostEstimate(flops=10**10, bytes_accessed=10**7, transcendentals=0),
        name="scores",
    )(grid, low, high, templates, far, core_far, *[jnp.asarray(t) for t in tables()])


def solution(mesh):
    placed = (P("tx", "ty", None), P("rot", None, None))
    return jax.shard_map(
        local, mesh=mesh, in_specs=placed, out_specs=(P("tx", "ty"), P("tx", "ty")), check_vma=False
    )
```

```python
import functools
import math

import jax
import jax.numpy as jnp
import ml_dtypes
import numpy as np
from jax import lax
from jax.experimental import pallas as pl
from jax.experimental.pallas import tpu as pltpu
from jax.sharding import PartitionSpec as P

RADIUS = 15
EPSILON = 1e-05
GRID = 64
BOX = 32
HALF = 16
LANES = 128
F32 = jnp.float32
BF16 = jnp.bfloat16


def halves(table):
    hi = table.astype(ml_dtypes.bfloat16)
    lo = (table - hi.astype(np.float64)).astype(ml_dtypes.bfloat16)
    return hi, lo


def wave(out_pos, in_pos):
    angle = 2.0 * np.pi / GRID * np.outer(out_pos, in_pos)
    return np.cos(angle), np.sin(angle)


def left_table(out_pos, in_pos, scale):
    cos, sin = wave(out_pos, in_pos)
    hi, lo = halves(np.concatenate([cos, sin], axis=0) * scale)
    return np.concatenate([hi, hi, lo], axis=1)


def sphere_np():
    centred = np.arange(BOX) - (BOX - 1) / 2.0
    sq = centred[:, None, None] ** 2 + centred[None, :, None] ** 2 + centred[None, None, :] ** 2
    return (sq <= float(RADIUS * RADIUS)).astype(np.float64)


def block(rows, cols, parts):
    some = next(iter(parts.values()))
    full = np.zeros((rows, cols) + some.shape)
    for at, part in parts.items():
        full[at] = part
    return full.transpose(0, 2, 1, 3).reshape(rows * some.shape[0], cols * some.shape[1])


@functools.cache
def tables():
    freq = np.arange(GRID)
    odd = np.arange(BOX) + 0.5
    centre = (BOX - 1) / 2.0
    cz, sz = wave(np.arange(GRID), odd)
    tomo = {}
    for kind in range(2):
        for side in range(2):
            for dup in range(2):
                tomo[2 * kind + side, 8 * side + 2 * dup + kind] = cz
                tomo[2 * kind + side, 8 * side + 4 + 2 * dup + kind] = -sz
    tomo_z = block(4, 16, tomo)
    ct, st = wave(np.arange(BOX), odd)
    kern = {}
    for rot in range(4):
        for jj in range(2):
            kern[2 * rot + jj, 8 * jj + rot] = ct
            kern[2 * rot + jj, 8 * jj + 4 + rot] = st
    kern_z = block(8, 16, kern)
    ci, si = wave(odd, np.arange(BOX))
    cm, sm = wave(odd, np.arange(BOX) + centre)
    back, back_mask = {}, {}
    for vol in range(4):
        back[vol, vol] = ci / BOX
        back[4 + vol, vol] = -si / BOX
    for vol in range(2):
        for copy in range(4):
            back_mask[vol, 4 * vol + copy] = cm / BOX
            back_mask[4 + vol, 4 * vol + copy] = -sm / BOX
    back_hi, back_lo = halves(block(8, 4, back))
    back_mask_z = block(8, 8, back_mask)
    sphere = sphere_np()
    shifted = np.arange(BOX) - centre
    cx, sx = wave(freq, shifted)
    cy, sy = wave(freq, np.arange(BOX))
    co, so = wave(odd, shifted)
    spec = np.einsum("ai,bj,ck,ijk->bac", cx + 1j * sx, cy + 1j * sy, co + 1j * so, sphere, optimize=True)
    mask_re = np.tile(spec.real, (1, 1, 4)).astype(np.float32)
    mask_im = np.tile(spec.imag, (1, 1, 4)).astype(np.float32)
    mask = sphere.reshape(BOX, BOX * BOX).astype(np.float32)
    scale = 1.0 / (GRID * GRID)
    return (
        mask,
        mask_re,
        mask_im,
        *halves(tomo_z),
        *halves(kern_z),
        left_table(freq, np.arange(GRID), 1.0),
        left_table(freq, np.arange(BOX), 1.0),
        left_table(np.arange(BOX), freq, scale),
        left_table(np.arange(BOX) + centre, freq, scale),
        np.concatenate([back_hi, back_lo], axis=1),
        back_hi,
        *halves(back_mask_z),
    )


def split(x):
    hi = x.astype(BF16)
    return hi, (x - hi.astype(F32)).astype(BF16)


def dot(a, b):
    return jnp.dot(a, b, preferred_element_type=F32)


def right_dot(x, w_hi, w_lo):
    hi, lo = split(x)
    return dot(hi, w_hi) + dot(lo, w_hi) + dot(hi, w_lo)


def left_dot(table, x, sign):
    hi, lo = split(x)
    out = dot(table, jnp.concatenate([hi, lo, hi], axis=0))
    n = out.shape[0] // 2
    tr, ti, br, bi = out[:n, :LANES], out[:n, LANES:], out[n:, :LANES], out[n:, LANES:]
    if sign > 0:
        return tr - bi, ti + br
    return tr + bi, ti - br


def add(a, b):
    return a[0] + b[0], a[1] + b[1]


def sub(a, b):
    return a[0] - b[0], a[1] - b[1]


def turn(a, sign):
    return (-a[1], a[0]) if sign > 0 else (a[1], -a[0])


def add_turned(a, b, sign):
    return (a[0] - b[1], a[1] + b[0]) if sign > 0 else (a[0] + b[1], a[1] - b[0])


def twiddle(a, num, den):
    num = num % den
    if num == 0:
        return a
    c, s = math.cos(2 * math.pi * num / den), math.sin(2 * math.pi * num / den)
    if 4 * num % den == 0:
        quarter = 4 * num // den
        return [a, turn(a, 1), (-a[0], -a[1]), turn(a, -1)][quarter]
    if 8 * num % den == 0:
        h = math.sqrt(0.5)
        odd = 8 * num // den
        if odd == 1:
            return (a[0] - a[1]) * h, (a[0] + a[1]) * h
        if odd == 3:
            return (a[0] + a[1]) * -h, (a[0] - a[1]) * h
        if odd == 5:
            return (a[1] - a[0]) * h, (a[0] + a[1]) * -h
        return (a[0] + a[1]) * h, (a[1] - a[0]) * h
    return a[0] * c - a[1] * s, a[0] * s + a[1] * c


def four(x, sign):
    a, b, c, d = add(x[0], x[2]), sub(x[0], x[2]), add(x[1], x[3]), sub(x[1], x[3])
    return [add(a, c), add_turned(b, d, sign), sub(a, c), add_turned(b, d, -sign)]


def eight(x, sign, keep=8):
    even, odd = four(x[0::2], sign), four(x[1::2], sign)
    odd = [odd[0], twiddle(odd[1], sign, 8), odd[2], twiddle(odd[3], 3 * sign, 8)]
    low = [add(even[0], odd[0]), add(even[1], odd[1]), add_turned(even[2], odd[2], sign), add(even[3], odd[3])]
    if keep == 4:
        return low
    return low + [sub(even[0], odd[0]), sub(even[1], odd[1]), add_turned(even[2], odd[2], -sign), sub(even[3], odd[3])]


def eight_of_four(x, sign):
    even = four(x, sign)
    odd = four([twiddle(x[m], sign * m, 8) for m in range(4)], sign)
    return [part for pair in zip(even, odd) for part in pair]


def prep(*refs):
    rotations, (mask_ref, kz_hi, kz_lo, ker_ref, out_ref) = refs[:4], refs[4:]
    filled = float(sphere_np().sum())
    low_half = lax.broadcasted_iota(jnp.int32, (1, LANES), 1) < GRID
    mask = mask_ref[...]
    normed = []
    for ref in rotations:
        t = ref[...]
        mu = jnp.sum(jnp.sum(t * mask, axis=0, keepdims=True), axis=1, keepdims=True) / filled
        d = (t - mu) * mask
        v = jnp.sum(jnp.sum(d * d, axis=0, keepdims=True), axis=1, keepdims=True) / filled
        normed.append(d * (1.0 / jnp.sqrt(v + EPSILON)))
    rows = []
    for jg in range(8):
        tile = [t[:, LANES * jg : LANES * (jg + 1)] for t in normed]
        far = [pltpu.roll(t, GRID, 1) for t in tile]
        rows += [
            jnp.concatenate([jnp.where(low_half, tile[r], far[r + 1]) for r in (0, 2)], axis=1),
            jnp.concatenate([jnp.where(low_half, far[r], tile[r + 1]) for r in (0, 2)], axis=1),
        ]
    out = right_dot(jnp.concatenate(rows, axis=0), kz_hi[...], kz_lo[...])
    for j in range(BOX):
        x = out[BOX * (j // 2) : BOX * (j // 2 + 1), 256 * (j % 2) : 256 * (j % 2 + 1)]
        re, im = left_dot(ker_ref[...], x, 1)
        out_ref[0, j] = re
        out_ref[1, j] = im


def get(ref, *index):
    return ref[(0,) + index], ref[(1,) + index]


def put(ref, value, *index):
    ref[(0,) + index] = value[0]
    ref[(1,) + index] = value[1]


def body(
    own_ref, before_ref, after_ref, kern_a, kern_b,
    mask_re, mask_im, tz_hi, tz_lo, fwd_ref, inv_ref, inv_m_ref, bz_two, bz_hi, bm_hi, bm_lo,
    top_ref, next_ref,
    spec, kspec, fspec, work, back, u_hi, u_lo,
):
    filled = float(sphere_np().sum())
    lane = lax.broadcasted_iota(jnp.int32, (1, LANES), 1)
    odd_quarter = lane % GRID >= BOX

    def tile(step):
        return pl.ds(pl.multiple_of(step * 8, 8), 8)

    def kernels_along_y(step):
        at = tile(step)
        for g, kern in enumerate((kern_a, kern_b)):
            for n2 in range(8):
                x = eight_of_four([get(kern, n2 + 8 * m, at) for m in range(4)], 1)
                for k1 in range(8):
                    put(work.at[g], twiddle(x[k1], n2 * k1, GRID), k1, n2)
            for k1 in range(8):
                x = eight([get(work.at[g], k1, n2) for n2 in range(8)], 1)
                for k2 in range(8):
                    put(kspec.at[g], x[k2], k1 + 8 * k2, at)

    for ref, first, count in ((before_ref, 0, HALF), (own_ref, HALF, BOX), (after_ref, HALF + BOX, HALF)):

        @pl.loop(0, count // 8)
        def _(step, ref=ref, first=first):
            y = step * 8
            rows = ref[pl.ds(y, 8)].reshape(8 * BOX, LANES)
            out = right_dot(jnp.concatenate([rows, rows * rows], axis=1), tz_hi[...], tz_lo[...])
            for e in range(8):
                some = out[BOX * e : BOX * (e + 1)]
                re, im = left_dot(fwd_ref[...], jnp.concatenate([some[:, :256], some[:, 256:]], axis=0), -1)
                spec[0, first + y + e] = re
                spec[1, first + y + e] = im
            kernels_along_y(step + first // 8)

    def finish(place, at, slot):
        for n2 in range(8):
            x = eight([get(work.at[slot], n2, k1) for k1 in range(8)], 1, keep=4)
            for n1 in range(4):
                put(back.at[place], x[n1], n2 + 8 * n1, at)

    @pl.loop(0, 8)
    def _(step):
        at = tile(step)
        for n2 in range(8):
            x = eight([get(spec, n2 + 8 * m, at) for m in range(8)], -1)
            for k1 in range(8):
                put(work.at[0], twiddle(x[k1], -n2 * k1, GRID), k1, n2)
        for k1 in range(8):
            x = eight([get(work.at[0], k1, n2) for n2 in range(8)], -1)
            prod = []
            for k2 in range(8):
                k = k1 + 8 * k2
                re, im = x[k2]
                put(fspec, [jnp.where(odd_quarter, pltpu.roll(v, BOX, 1), v) for v in (re, im)], k, at)
                a, b = mask_re[k, at], mask_im[k, at]
                prod.append((re * a - im * b, re * b + im * a))
            prod = eight(prod, 1)
            for n2 in range(8):
                put(work.at[1], twiddle(prod[n2], k1 * n2, GRID), n2, k1)
        finish(2, at, 1)

    def product_along_y(step, g):
        at = tile(step)
        for k1 in range(8):
            prod = []
            for k2 in range(8):
                k = k1 + 8 * k2
                a, b = get(fspec, k, at)
                re, im = get(kspec.at[g], k, at)
                prod.append((re * a - im * b, re * b + im * a))
            prod = eight(prod, 1)
            for n2 in range(8):
                put(work.at[g], twiddle(prod[n2], k1 * n2, GRID), n2, k1)
        finish(g, at, g)

    def along_x(step, s):
        for yy in range(4):
            y = 4 * step + yy
            x = jnp.concatenate([back[s, 0, y], back[s, 1, y]], axis=1)
            hi, lo = split(jnp.concatenate(left_dot(inv_ref[...] if s < 2 else inv_m_ref[...], x, 1), axis=1))
            rows = pl.ds(pl.multiple_of(y * BOX, BOX), BOX)
            u_hi[s, rows, :] = hi
            u_lo[s, rows, :] = lo

    @pl.loop(0, 8)
    def _(step):
        product_along_y(step, 0)
        along_x(step, 2)

    @pl.loop(0, 8)
    def _(step):
        product_along_y(step, 1)
        along_x(step, 0)

    for step in range(8):
        along_x(step, 1)

    def merged(one, other):
        return jnp.maximum(one[0], other[0]), jnp.maximum(jnp.minimum(one[0], other[0]), jnp.maximum(one[1], other[1]))

    quarter = lane // BOX
    for part in range(2):
        rows = pl.ds(512 * part, 512)
        hi, lo = u_hi[2, rows, :], u_lo[2, rows, :]
        sums = dot(hi, bm_hi[...]) + dot(lo, bm_hi[...]) + dot(hi, bm_lo[...])
        mean = sums[:, :LANES] / filled
        var = jnp.maximum(sums[:, LANES:] / filled - mean * mean, 0.0)
        scale = 1.0 / (np.float32(np.sqrt(filled)) * jnp.sqrt(var + EPSILON))
        corr = []
        for g in range(2):
            both = dot(u_hi[g, rows, :], bz_two[...])
            corr.append((both[:, :LANES] + both[:, LANES:] + dot(u_lo[g, rows, :], bz_hi[...])) * scale)
        best = jnp.maximum(corr[0], corr[1]), jnp.minimum(corr[0], corr[1])
        best = merged(best, [pltpu.roll(v, GRID, 1) for v in best])
        best = merged(best, [pltpu.roll(v, BOX, 1) for v in best])
        for ref, v in zip((top_ref, next_ref), best):
            for e in range(4):
                y = [v[BOX * (4 * e + q) : BOX * (4 * e + q + 1)] for q in range(4)]
                o = jnp.where(quarter < 2, jnp.where(quarter == 0, y[0], y[1]), jnp.where(quarter == 2, y[2], y[3]))
                ref[:, LANES * (4 * part + e) : LANES * (4 * part + e + 1)] = o


def shifts(count, step):
    return [(i, i + step) for i in range(count) if 0 <= i + step < count]


def local(tomogram, templates):
    tx, ty, rots = lax.axis_size("tx"), lax.axis_size("ty"), lax.axis_size("rot")
    tile = jnp.swapaxes(tomogram, 0, 1)

    def pack(part):
        return jnp.concatenate([part[:HALF], part[HALF:]], axis=2)

    def unpack(part):
        return jnp.concatenate([part[:, :, :GRID], part[:, :, GRID:]], axis=0)

    before = lax.ppermute(pack(tile[:, HALF:]), "tx", shifts(tx, 1))
    after = lax.ppermute(pack(tile[:, :HALF]), "tx", shifts(tx, -1))

    core = lax.rem(lax.axis_index("ty"), 2)
    mine = lax.dynamic_slice_in_dim(templates, core, 1, axis=0)
    far = [lax.ppermute(mine, "rot", [(i, (i + s) % rots) for i in range(rots)]) for s in range(1, rots)]
    far = jnp.concatenate(far, axis=0)
    core_far = lax.ppermute(far, "ty", [(i, i + 1 - 2 * (i % 2)) for i in range(ty)])

    grid = jnp.concatenate(
        [
            jnp.concatenate([unpack(before), tile[:, :HALF]], axis=1),
            jnp.concatenate([tile[:, HALF:], unpack(after)], axis=1),
        ],
        axis=2,
    )
    low = lax.ppermute(grid[HALF:], "ty", shifts(ty, 1))
    high = lax.ppermute(grid[:HALF], "ty", shifts(ty, -1))
    first = prep_call(templates[0], templates[1], far[0], far[1])
    second = prep_call(far[2], core_far[0], core_far[1], core_far[2])
    return kernel_call(grid, low, high, first, second)


def prep_call(*four_templates):
    mask, _, _, _, _, kz_hi, kz_lo, _, ker = tables()[:9]
    return pl.pallas_call(
        prep,
        out_shape=jax.ShapeDtypeStruct((2, BOX, GRID, LANES), F32),
        compiler_params=pltpu.CompilerParams(vmem_limit_bytes=16 * 1024 * 1024),
        cost_estimate=pl.CostEstimate(flops=2 * 10**9, bytes_accessed=4 * 10**6, transcendentals=0),
        name="prep",
    )(*four_templates, *[jnp.asarray(t) for t in (mask, kz_hi, kz_lo, ker)])


def kernel_call(grid, low, high, first, second):
    out = jax.ShapeDtypeStruct((BOX, BOX * BOX), F32)
    scratch = [
        pltpu.VMEM((2, GRID, GRID, LANES), F32),
        pltpu.VMEM((2, 2, GRID, GRID, LANES), F32),
        pltpu.VMEM((2, GRID, GRID, LANES), F32),
        pltpu.VMEM((2, 2, 8, 8, 8, LANES), F32),
        pltpu.VMEM((3, 2, BOX, GRID, LANES), F32),
        pltpu.VMEM((3, BOX * BOX, 2 * LANES), BF16),
        pltpu.VMEM((3, BOX * BOX, 2 * LANES), BF16),
    ]
    _, mask_re, mask_im, tz_hi, tz_lo, _, _, fwd, _, inv, inv_m, *back = tables()
    return pl.pallas_call(
        body,
        out_shape=(out, out),
        scratch_shapes=scratch,
        compiler_params=pltpu.CompilerParams(vmem_limit_bytes=40 * 1024 * 1024),
        cost_estimate=pl.CostEstimate(flops=10**10, bytes_accessed=10**7, transcendentals=0),
        name="scores",
    )(grid, low, high, first, second, *[jnp.asarray(t) for t in (mask_re, mask_im, tz_hi, tz_lo, fwd, inv, inv_m, *back)])


def solution(mesh):
    placed = (P("tx", "ty", None), P("rot", None, None))
    return jax.shard_map(
        local, mesh=mesh, in_specs=placed, out_specs=(P("tx", "ty"), P("tx", "ty")), check_vma=False
    )
```

```python
import functools
import math

import jax
import jax.numpy as jnp
import ml_dtypes
import numpy as np
from jax import lax
from jax.experimental import pallas as pl
from jax.experimental.pallas import tpu as pltpu
from jax.sharding import PartitionSpec as P

RADIUS = 15
EPSILON = 1e-05
GRID = 64
BOX = 32
HALF = 16
LANES = 128
F32 = jnp.float32
BF16 = jnp.bfloat16


def halves(table):
    hi = table.astype(ml_dtypes.bfloat16)
    lo = (table - hi.astype(np.float64)).astype(ml_dtypes.bfloat16)
    return hi, lo


def wave(out_pos, in_pos):
    angle = 2.0 * np.pi / GRID * np.outer(out_pos, in_pos)
    return np.cos(angle), np.sin(angle)


def left_table(out_pos, in_pos, scale):
    cos, sin = wave(out_pos, in_pos)
    hi, lo = halves(np.concatenate([cos, sin], axis=0) * scale)
    return np.concatenate([hi, hi, lo], axis=1)


def sphere_np():
    centred = np.arange(BOX) - (BOX - 1) / 2.0
    sq = centred[:, None, None] ** 2 + centred[None, :, None] ** 2 + centred[None, None, :] ** 2
    return (sq <= float(RADIUS * RADIUS)).astype(np.float64)


def block(rows, cols, parts):
    some = next(iter(parts.values()))
    full = np.zeros((rows, cols) + some.shape)
    for at, part in parts.items():
        full[at] = part
    return full.transpose(0, 2, 1, 3).reshape(rows * some.shape[0], cols * some.shape[1])


@functools.cache
def tables():
    freq = np.arange(GRID)
    odd = np.arange(BOX) + 0.5
    centre = (BOX - 1) / 2.0
    cz, sz = wave(np.arange(GRID), odd)
    tomo = {}
    for kind in range(2):
        for dup in range(2):
            tomo[kind, 2 * dup + kind] = cz
            tomo[kind, 4 + 2 * dup + kind] = -sz
    tomo_hi, tomo_lo = halves(block(2, 8, tomo))
    ct, st = wave(np.arange(BOX), odd)
    kern = {}
    for rot in range(4):
        for jj in range(2):
            kern[2 * rot + jj, 8 * jj + rot] = ct
            kern[2 * rot + jj, 8 * jj + 4 + rot] = st
    kern_z = block(8, 16, kern)
    ci, si = wave(odd, np.arange(BOX))
    cm, sm = wave(odd, np.arange(BOX) + centre)
    back, back_mask = {}, {}
    for vol in range(4):
        back[vol, vol] = ci / BOX
        back[4 + vol, vol] = -si / BOX
    for row in range(4):
        for copy in range(4):
            back_mask[row, 4 * (row % 2) + copy] = cm / BOX
            back_mask[4 + row, 4 * (row % 2) + copy] = -sm / BOX
    back_hi, back_lo = halves(block(8, 4, back))
    back_mask_z = block(8, 8, back_mask)
    one = np.eye(BOX)
    copies = block(8, 8, {(row, col): one for half in (0, 4) for row, first in ((half, 0), (half + 2, 4)) for col in range(first, first + 4)})
    sphere = sphere_np()
    shifted = np.arange(BOX) - centre
    cx, sx = wave(freq, shifted)
    cy, sy = wave(freq, np.arange(BOX))
    co, so = wave(odd, shifted)
    spec = np.einsum("ai,bj,ck,ijk->bac", cx + 1j * sx, cy + 1j * sy, co + 1j * so, sphere, optimize=True)
    spec = np.concatenate([spec[:, :BOX], spec[:, :BOX], spec[:, BOX:], spec[:, BOX:]], axis=2)
    mask_re, mask_im = spec.real.astype(np.float32), spec.imag.astype(np.float32)
    mask = sphere.reshape(BOX, BOX * BOX).astype(np.float32)
    scale = 1.0 / (GRID * GRID)
    return (
        mask,
        mask_re,
        mask_im,
        np.concatenate([tomo_hi, tomo_hi], axis=0),
        tomo_lo,
        *halves(kern_z),
        left_table(freq[:BOX], np.arange(GRID), 1.0),
        left_table(freq, np.arange(BOX), 1.0),
        left_table(np.arange(BOX), freq, scale),
        np.concatenate([left_table(np.arange(BOX) + centre, f, scale) for f in (freq[:BOX], freq[BOX:])], axis=0),
        np.concatenate([back_hi, back_lo], axis=1),
        back_hi,
        *halves(back_mask_z),
        copies.astype(ml_dtypes.bfloat16),
    )


def split(x):
    hi = x.astype(BF16)
    return hi, (x - hi.astype(F32)).astype(BF16)


def dot(a, b):
    return jnp.dot(a, b, preferred_element_type=F32)


def right_dot(x, w_hi, w_lo):
    hi, lo = split(x)
    return dot(hi, w_hi) + dot(lo, w_hi) + dot(hi, w_lo)


def left_dot(table, x, sign):
    hi, lo = split(x)
    return joined_parts(dot(table, jnp.concatenate([hi, lo, hi], axis=0)), sign)


def joined_parts(out, sign):
    n = out.shape[0] // 2
    tr, ti, br, bi = out[:n, :LANES], out[:n, LANES:], out[n:, :LANES], out[n:, LANES:]
    if sign > 0:
        return tr - bi, ti + br
    return tr + bi, ti - br


def add(a, b):
    return a[0] + b[0], a[1] + b[1]


def sub(a, b):
    return a[0] - b[0], a[1] - b[1]


def turn(a, sign):
    return (-a[1], a[0]) if sign > 0 else (a[1], -a[0])


def add_turned(a, b, sign):
    return (a[0] - b[1], a[1] + b[0]) if sign > 0 else (a[0] + b[1], a[1] - b[0])


def twiddle(a, num, den):
    num = num % den
    if num == 0:
        return a
    c, s = math.cos(2 * math.pi * num / den), math.sin(2 * math.pi * num / den)
    if 4 * num % den == 0:
        quarter = 4 * num // den
        return [a, turn(a, 1), (-a[0], -a[1]), turn(a, -1)][quarter]
    if 8 * num % den == 0:
        h = math.sqrt(0.5)
        odd = 8 * num // den
        if odd == 1:
            return (a[0] - a[1]) * h, (a[0] + a[1]) * h
        if odd == 3:
            return (a[0] + a[1]) * -h, (a[0] - a[1]) * h
        if odd == 5:
            return (a[1] - a[0]) * h, (a[0] + a[1]) * -h
        return (a[0] + a[1]) * h, (a[1] - a[0]) * h
    return a[0] * c - a[1] * s, a[0] * s + a[1] * c


def four(x, sign):
    a, b, c, d = add(x[0], x[2]), sub(x[0], x[2]), add(x[1], x[3]), sub(x[1], x[3])
    return [add(a, c), add_turned(b, d, sign), sub(a, c), add_turned(b, d, -sign)]


def eight(x, sign, keep=8):
    even, odd = four(x[0::2], sign), four(x[1::2], sign)
    odd = [odd[0], twiddle(odd[1], sign, 8), odd[2], twiddle(odd[3], 3 * sign, 8)]
    low = [add(even[0], odd[0]), add(even[1], odd[1]), add_turned(even[2], odd[2], sign), add(even[3], odd[3])]
    if keep == 4:
        return low
    return low + [sub(even[0], odd[0]), sub(even[1], odd[1]), add_turned(even[2], odd[2], -sign), sub(even[3], odd[3])]


def eight_of_four(x, sign):
    even = four(x, sign)
    odd = four([twiddle(x[m], sign * m, 8) for m in range(4)], sign)
    return [part for pair in zip(even, odd) for part in pair]


def prep(*refs):
    rotations, (mask_ref, kz_hi, kz_lo, ker_ref, out_ref) = refs[:4], refs[4:]
    filled = float(sphere_np().sum())
    low_half = lax.broadcasted_iota(jnp.int32, (1, LANES), 1) < GRID
    mask = mask_ref[...]
    normed = []
    for ref in rotations:
        t = ref[...]
        mu = jnp.sum(jnp.sum(t * mask, axis=0, keepdims=True), axis=1, keepdims=True) / filled
        d = (t - mu) * mask
        v = jnp.sum(jnp.sum(d * d, axis=0, keepdims=True), axis=1, keepdims=True) / filled
        normed.append(d * (1.0 / jnp.sqrt(v + EPSILON)))
    rows = []
    for jg in range(8):
        tile = [t[:, LANES * jg : LANES * (jg + 1)] for t in normed]
        far = [pltpu.roll(t, GRID, 1) for t in tile]
        rows += [
            jnp.concatenate([jnp.where(low_half, tile[r], far[r + 1]) for r in (0, 2)], axis=1),
            jnp.concatenate([jnp.where(low_half, far[r], tile[r + 1]) for r in (0, 2)], axis=1),
        ]
    out = right_dot(jnp.concatenate(rows, axis=0), kz_hi[...], kz_lo[...])
    for j in range(BOX):
        x = out[BOX * (j // 2) : BOX * (j // 2 + 1), 256 * (j % 2) : 256 * (j % 2 + 1)]
        re, im = left_dot(ker_ref[...], x, 1)
        out_ref[0, j] = re
        out_ref[1, j] = im


def get(ref, *index):
    return ref[(0,) + index], ref[(1,) + index]


def put(ref, value, *index):
    ref[(0,) + index] = value[0]
    ref[(1,) + index] = value[1]


def body(
    own_ref, before_ref, after_ref, kern_a, kern_b,
    mask_re, mask_im, tz_two, tz_lo, fwd_ref, inv_ref, inv_m_ref, bz_two, bz_hi, bm_hi, bm_lo, copies_ref,
    top_ref, next_ref,
    spec, kspec, fspec, work, slab, back, back_m, plain, u_hi, u_lo,
):
    filled = float(sphere_np().sum())
    lane = lax.broadcasted_iota(jnp.int32, (1, LANES), 1)
    odd_quarter = lane % GRID >= BOX

    def tile(step):
        return pl.ds(pl.multiple_of(step * 8, 8), 8)

    def kernels_first(at, n2, slot):
        for g, kern in enumerate((kern_a, kern_b)):
            x = eight_of_four([get(kern, n2 + 8 * m, at) for m in range(4)], 1)
            for k1 in range(8):
                put(work.at[2 * slot + g], twiddle(x[k1], n2 * k1, GRID), k1, n2)

    def kernels_second(at, k1, slot):
        for g in range(2):
            x = eight([get(work.at[2 * slot + g], k1, n2) for n2 in range(8)], 1)
            for k2 in range(8):
                put(kspec.at[g], x[k2], k1 + 8 * k2, at)

    low_half = lane < GRID
    row_odd = lax.broadcasted_iota(jnp.int32, (GRID, 2 * LANES), 0) % 2 == 1
    col_upper = lax.broadcasted_iota(jnp.int32, (GRID, 2 * LANES), 1) % LANES >= GRID
    parity = jnp.where(jnp.logical_and(row_odd, col_upper), -1.0, 1.0).astype(F32)
    def along_z(step):
        ref, start = ((before_ref, 0), (own_ref, 2), (after_ref, 6))[(step >= 2) + (step >= 6)]
        one = ref[8 * (step - start) : 8 * (step - start) + 8].reshape(8 * BOX, LANES)
        two = one * one
        lower = jnp.where(low_half, one, pltpu.roll(two, GRID, 1))
        upper = jnp.where(low_half, pltpu.roll(one, GRID, 1), two)
        rows = [v[BOX * e : BOX * (e + 1)] for e in range(8) for v in (lower, upper)]
        hi, lo = split(jnp.concatenate(rows, axis=0))
        slab[step % 2] = dot(jnp.concatenate([hi, lo], axis=1), tz_two[...]) + dot(hi, tz_lo[...])

    along_z(0)
    for step in range(8):
        at = slice(8 * step, 8 * step + 8)
        if step < 7:
            along_z(step + 1)
        for e in range(8):
            kernels_first(at, e, step % 2)
        for e in range(8):
            re, im = left_dot(fwd_ref[...], slab[step % 2, GRID * e : GRID * (e + 1)] * parity, -1)
            spec[0, 8 * step + e] = re
            spec[1, 8 * step + e] = im
            kernels_second(at, e, step % 2)

    def finish(place, at, slot):
        for n2 in range(8):
            x = eight([get(work.at[slot], n2, k1) for k1 in range(8)], 1, keep=4)
            for n1 in range(4):
                put(place, x[n1], n2 + 8 * n1, at)

    @pl.loop(0, 4)
    def _(step):
        at = tile(step)
        for n2 in range(8):
            x = eight([get(spec, n2 + 8 * m, at) for m in range(8)], -1)
            for k1 in range(8):
                put(work.at[0], twiddle(x[k1], -n2 * k1, GRID), k1, n2)
        for k1 in range(8):
            x = eight([get(work.at[0], k1, n2) for n2 in range(8)], -1)
            prod = []
            for k2 in range(8):
                k = k1 + 8 * k2
                re, im = x[k2]
                put(plain, (re, im), k)
                a, b = mask_re[k, at], mask_im[k, at]
                prod.append((re * a - im * b, re * b + im * a))
            prod = eight(prod, 1)
            for n2 in range(8):
                put(work.at[1], twiddle(prod[n2], k1 * n2, GRID), n2, k1)
        for c in range(2):
            out = dot(jnp.concatenate(split(plain[c].reshape(GRID * 8, LANES)), axis=1), copies_ref[...])
            fspec[c, :, at] = out[:, :LANES].reshape(GRID, 8, LANES)
            fspec[c, :, tile(step + 4)] = out[:, LANES:].reshape(GRID, 8, LANES)
        finish(back_m, at, 1)

    def product_along_y(at, g, k1):
        prod = []
        for k2 in range(8):
            k = k1 + 8 * k2
            a, b = get(fspec, k, at)
            re, im = get(kspec.at[g], k, at)
            prod.append((re * a - im * b, re * b + im * a))
        prod = eight(prod, 1)
        for n2 in range(8):
            put(work.at[g], twiddle(prod[n2], k1 * n2, GRID), n2, k1)

    def along_x(y, s):
        if s == 2:
            hi, lo = split(jnp.concatenate([back_m[0, y], back_m[1, y]], axis=1))
            out = dot(inv_m_ref[...], jnp.concatenate([hi, lo, hi], axis=0))
            first, other = joined_parts(out[: 2 * BOX], 1), joined_parts(out[2 * BOX :], 1)
            res = [jnp.where(low_half, a, b) for a, b in zip(first, other)]
        else:
            res = left_dot(inv_ref[...], jnp.concatenate([back[s, 0, y], back[s, 1, y]], axis=1), 1)
        hi, lo = split(jnp.concatenate(res, axis=1))
        rows = pl.ds(pl.multiple_of(y * BOX, BOX), BOX)
        u_hi[s, rows, :] = hi
        u_lo[s, rows, :] = lo

    for g, s in ((0, 2), (1, 0)):

        @pl.loop(0, 8, unroll=4)
        def _(step, g=g, s=s):
            at = tile(step)
            for k1 in range(8):
                product_along_y(at, g, k1)
                if k1 % 2:
                    along_x(4 * step + k1 // 2, s)
            finish(back.at[g], at, g)

    for y in range(BOX):
        along_x(y, 1)

    def merged(one, other):
        return jnp.maximum(one[0], other[0]), jnp.maximum(jnp.minimum(one[0], other[0]), jnp.maximum(one[1], other[1]))

    quarter = lane // BOX
    for part in range(2):
        rows = pl.ds(512 * part, 512)
        hi, lo = u_hi[2, rows, :], u_lo[2, rows, :]
        sums = dot(hi, bm_hi[...]) + dot(lo, bm_hi[...]) + dot(hi, bm_lo[...])
        mean = sums[:, :LANES] / filled
        var = jnp.maximum(sums[:, LANES:] / filled - mean * mean, 0.0)
        scale = 1.0 / (np.float32(np.sqrt(filled)) * jnp.sqrt(var + EPSILON))
        corr = []
        for g in range(2):
            both = dot(u_hi[g, rows, :], bz_two[...])
            corr.append((both[:, :LANES] + both[:, LANES:] + dot(u_lo[g, rows, :], bz_hi[...])) * scale)
        best = jnp.maximum(corr[0], corr[1]), jnp.minimum(corr[0], corr[1])
        best = merged(best, [pltpu.roll(v, GRID, 1) for v in best])
        best = merged(best, [pltpu.roll(v, BOX, 1) for v in best])
        for ref, v in zip((top_ref, next_ref), best):
            for e in range(4):
                y = [v[BOX * (4 * e + q) : BOX * (4 * e + q + 1)] for q in range(4)]
                o = jnp.where(quarter < 2, jnp.where(quarter == 0, y[0], y[1]), jnp.where(quarter == 2, y[2], y[3]))
                ref[:, LANES * (4 * part + e) : LANES * (4 * part + e + 1)] = o


def shifts(count, step):
    return [(i, i + step) for i in range(count) if 0 <= i + step < count]


def local(tomogram, templates):
    tx, ty, rots = lax.axis_size("tx"), lax.axis_size("ty"), lax.axis_size("rot")
    tile = jnp.swapaxes(tomogram, 0, 1)

    def pack(part):
        return jnp.concatenate([part[:HALF], part[HALF:]], axis=2)

    def unpack(part):
        return jnp.concatenate([part[:, :, :GRID], part[:, :, GRID:]], axis=0)

    before = lax.ppermute(pack(tile[:, HALF:]), "tx", shifts(tx, 1))
    after = lax.ppermute(pack(tile[:, :HALF]), "tx", shifts(tx, -1))

    core = lax.rem(lax.axis_index("ty"), 2)
    mine = lax.dynamic_slice_in_dim(templates, core, 1, axis=0)
    far = [lax.ppermute(mine, "rot", [(i, (i + s) % rots) for i in range(rots)]) for s in range(1, rots)]
    far = jnp.concatenate(far, axis=0)
    core_far = lax.ppermute(far, "ty", [(i, i + 1 - 2 * (i % 2)) for i in range(ty)])

    grid = jnp.concatenate(
        [
            jnp.concatenate([unpack(before), tile[:, :HALF]], axis=1),
            jnp.concatenate([tile[:, HALF:], unpack(after)], axis=1),
        ],
        axis=2,
    )
    low = lax.ppermute(grid[HALF:], "ty", shifts(ty, 1))
    high = lax.ppermute(grid[:HALF], "ty", shifts(ty, -1))
    first = prep_call(templates[0], templates[1], far[0], far[1])
    second = prep_call(far[2], core_far[0], core_far[1], core_far[2])
    return kernel_call(grid, low, high, first, second)


def prep_call(*four_templates):
    mask, _, _, _, _, kz_hi, kz_lo, _, ker = tables()[:9]
    return pl.pallas_call(
        prep,
        out_shape=jax.ShapeDtypeStruct((2, BOX, GRID, LANES), F32),
        compiler_params=pltpu.CompilerParams(vmem_limit_bytes=16 * 1024 * 1024),
        cost_estimate=pl.CostEstimate(flops=2 * 10**9, bytes_accessed=4 * 10**6, transcendentals=0),
        name="prep",
    )(*four_templates, *[jnp.asarray(t) for t in (mask, kz_hi, kz_lo, ker)])


def kernel_call(grid, low, high, first, second):
    out = jax.ShapeDtypeStruct((BOX, BOX * BOX), F32)
    scratch = [
        pltpu.VMEM((2, GRID, BOX, LANES), F32),
        pltpu.VMEM((2, 2, GRID, GRID, LANES), F32),
        pltpu.VMEM((2, GRID, GRID, LANES), F32),
        pltpu.VMEM((4, 2, 8, 8, 8, LANES), F32),
        pltpu.VMEM((2, 8 * GRID, 2 * LANES), F32),
        pltpu.VMEM((2, 2, BOX, GRID, LANES), F32),
        pltpu.VMEM((2, BOX, BOX, LANES), F32),
        pltpu.VMEM((2, GRID, 8, LANES), F32),
        pltpu.VMEM((3, BOX * BOX, 2 * LANES), BF16),
        pltpu.VMEM((3, BOX * BOX, 2 * LANES), BF16),
    ]
    _, mask_re, mask_im, tz_hi, tz_lo, _, _, fwd, _, inv, inv_m, *back = tables()
    return pl.pallas_call(
        body,
        out_shape=(out, out),
        scratch_shapes=scratch,
        compiler_params=pltpu.CompilerParams(vmem_limit_bytes=40 * 1024 * 1024),
        cost_estimate=pl.CostEstimate(flops=10**10, bytes_accessed=10**7, transcendentals=0),
        name="scores",
    )(grid, low, high, first, second, *[jnp.asarray(t) for t in (mask_re, mask_im, tz_hi, tz_lo, fwd, inv, inv_m, *back)])


def solution(mesh):
    placed = (P("tx", "ty", None), P("rot", None, None))
    return jax.shard_map(
        local, mesh=mesh, in_specs=placed, out_specs=(P("tx", "ty"), P("tx", "ty")), check_vma=False
    )
```

```python
import functools
import math

import jax
import jax.numpy as jnp
import ml_dtypes
import numpy as np
from jax import lax
from jax.experimental import pallas as pl
from jax.experimental.pallas import tpu as pltpu
from jax.sharding import PartitionSpec as P

RADIUS = 15
EPSILON = 1e-05
GRID = 64
BOX = 32
HALF = 16
LANES = 128
F32 = jnp.float32
BF16 = jnp.bfloat16


def halves(table):
    hi = table.astype(ml_dtypes.bfloat16)
    lo = (table - hi.astype(np.float64)).astype(ml_dtypes.bfloat16)
    return hi, lo


def stacked(table):
    hi, lo = halves(table)
    return np.concatenate([hi, hi, lo], axis=0)


def wave(out_pos, in_pos):
    angle = 2.0 * np.pi / GRID * np.outer(out_pos, in_pos)
    return np.cos(angle), np.sin(angle)


def left_table(out_pos, in_pos, scale):
    cos, sin = wave(out_pos, in_pos)
    hi, lo = halves(np.concatenate([cos, sin], axis=0) * scale)
    return np.concatenate([hi, hi, lo], axis=1)


def sphere_np():
    centred = np.arange(BOX) - (BOX - 1) / 2.0
    sq = centred[:, None, None] ** 2 + centred[None, :, None] ** 2 + centred[None, None, :] ** 2
    return (sq <= float(RADIUS * RADIUS)).astype(np.float64)


def block(rows, cols, parts):
    some = next(iter(parts.values()))
    full = np.zeros((rows, cols) + some.shape)
    for at, part in parts.items():
        full[at] = part
    return full.transpose(0, 2, 1, 3).reshape(rows * some.shape[0], cols * some.shape[1])


@functools.cache
def tables():
    freq = np.arange(GRID)
    odd = np.arange(BOX) + 0.5
    centre = (BOX - 1) / 2.0
    cz, sz = wave(np.arange(GRID), odd)
    tomo = {}
    for kind in range(2):
        for dup in range(2):
            tomo[kind, 2 * dup + kind] = cz
            tomo[kind, 4 + 2 * dup + kind] = -sz
    tomo_hi, tomo_lo = halves(block(2, 8, tomo))
    ct, st = wave(np.arange(BOX), odd)
    kern = {}
    for rot in range(4):
        for jj in range(2):
            kern[2 * rot + jj, 8 * jj + rot] = ct
            kern[2 * rot + jj, 8 * jj + 4 + rot] = st
    kern_z = block(8, 16, kern)
    ci, si = wave(odd, np.arange(BOX))
    cm, sm = wave(odd, np.arange(BOX) + centre)
    back, back_mask = {}, {}
    for vol in range(4):
        back[vol, vol] = ci / BOX
        back[4 + vol, vol] = -si / BOX
    for row in range(4):
        for copy in range(4):
            back_mask[row, 4 * (row % 2) + copy] = cm / BOX
            back_mask[4 + row, 4 * (row % 2) + copy] = -sm / BOX
    back_hi, back_lo = halves(block(8, 4, back))
    back_mask_z = block(8, 8, back_mask)
    one = np.eye(BOX)
    copies = block(8, 8, {(row, col): one for half in (0, 4) for row, first in ((half, 0), (half + 2, 4)) for col in range(first, first + 4)})
    sphere = sphere_np()
    shifted = np.arange(BOX) - centre
    cx, sx = wave(freq, shifted)
    cy, sy = wave(freq, np.arange(BOX))
    co, so = wave(odd, shifted)
    spec = np.einsum("ai,bj,ck,ijk->bac", cx + 1j * sx, cy + 1j * sy, co + 1j * so, sphere, optimize=True)
    spec = np.concatenate([spec[:, :BOX], spec[:, :BOX], spec[:, BOX:], spec[:, BOX:]], axis=2)
    mask_re, mask_im = spec.real.astype(np.float32), spec.imag.astype(np.float32)
    mask = sphere.reshape(BOX, BOX * BOX).astype(np.float32)
    scale = 1.0 / (GRID * GRID)
    return (
        mask,
        mask_re,
        mask_im,
        np.concatenate([tomo_hi, tomo_hi, tomo_lo], axis=0),
        stacked(kern_z),
        left_table(freq[:BOX], np.arange(GRID), 1.0),
        left_table(freq, np.arange(BOX), 1.0),
        left_table(np.arange(BOX), freq, scale),
        np.concatenate([left_table(np.arange(BOX) + centre, f, scale) for f in (freq[:BOX], freq[BOX:])], axis=0),
        np.concatenate([back_hi, back_lo], axis=1),
        back_hi,
        stacked(back_mask_z),
        copies.astype(ml_dtypes.bfloat16),
    )


def split(x):
    hi = x.astype(BF16)
    return hi, (x - hi.astype(F32)).astype(BF16)


def dot(a, b):
    return jnp.dot(a, b, preferred_element_type=F32)


def right_dot(hi, lo, table):
    return dot(jnp.concatenate([hi, lo, hi], axis=1), table)


def left_dot(table, x, sign):
    hi, lo = split(x)
    return joined_parts(dot(table, jnp.concatenate([hi, lo, hi], axis=0)), sign)


def joined_parts(out, sign):
    n = out.shape[0] // 2
    tr, ti, br, bi = out[:n, :LANES], out[:n, LANES:], out[n:, :LANES], out[n:, LANES:]
    if sign > 0:
        return tr - bi, ti + br
    return tr + bi, ti - br


def add(a, b):
    return a[0] + b[0], a[1] + b[1]


def sub(a, b):
    return a[0] - b[0], a[1] - b[1]


def turn(a, sign):
    return (-a[1], a[0]) if sign > 0 else (a[1], -a[0])


def add_turned(a, b, sign):
    return (a[0] - b[1], a[1] + b[0]) if sign > 0 else (a[0] + b[1], a[1] - b[0])


def twiddle(a, num, den):
    num = num % den
    if num == 0:
        return a
    c, s = math.cos(2 * math.pi * num / den), math.sin(2 * math.pi * num / den)
    if 4 * num % den == 0:
        quarter = 4 * num // den
        return [a, turn(a, 1), (-a[0], -a[1]), turn(a, -1)][quarter]
    if 8 * num % den == 0:
        h = math.sqrt(0.5)
        odd = 8 * num // den
        if odd == 1:
            return (a[0] - a[1]) * h, (a[0] + a[1]) * h
        if odd == 3:
            return (a[0] + a[1]) * -h, (a[0] - a[1]) * h
        if odd == 5:
            return (a[1] - a[0]) * h, (a[0] + a[1]) * -h
        return (a[0] + a[1]) * h, (a[1] - a[0]) * h
    return a[0] * c - a[1] * s, a[0] * s + a[1] * c


def four(x, sign):
    a, b, c, d = add(x[0], x[2]), sub(x[0], x[2]), add(x[1], x[3]), sub(x[1], x[3])
    return [add(a, c), add_turned(b, d, sign), sub(a, c), add_turned(b, d, -sign)]


def eight(x, sign, keep=8):
    even, odd = four(x[0::2], sign), four(x[1::2], sign)
    odd = [odd[0], twiddle(odd[1], sign, 8), odd[2], twiddle(odd[3], 3 * sign, 8)]
    low = [add(even[0], odd[0]), add(even[1], odd[1]), add_turned(even[2], odd[2], sign), add(even[3], odd[3])]
    if keep == 4:
        return low
    return low + [sub(even[0], odd[0]), sub(even[1], odd[1]), add_turned(even[2], odd[2], -sign), sub(even[3], odd[3])]


def eight_of_four(x, sign):
    even = four(x, sign)
    odd = four([twiddle(x[m], sign * m, 8) for m in range(4)], sign)
    return [part for pair in zip(even, odd) for part in pair]


def prep(*refs):
    rotations, (mask_ref, kz_ref, ker_ref, out_ref) = refs[:4], refs[4:]
    filled = float(sphere_np().sum())
    low_half = lax.broadcasted_iota(jnp.int32, (1, LANES), 1) < GRID
    mask = mask_ref[...]
    normed = []
    for ref in rotations:
        t = ref[...]
        mu = jnp.sum(jnp.sum(t * mask, axis=0, keepdims=True), axis=1, keepdims=True) / filled
        d = (t - mu) * mask
        v = jnp.sum(jnp.sum(d * d, axis=0, keepdims=True), axis=1, keepdims=True) / filled
        normed.append(d * (1.0 / jnp.sqrt(v + EPSILON)))
    rows = []
    for jg in range(8):
        tile = [t[:, LANES * jg : LANES * (jg + 1)] for t in normed]
        far = [pltpu.roll(t, GRID, 1) for t in tile]
        rows += [
            jnp.concatenate([jnp.where(low_half, tile[r], far[r + 1]) for r in (0, 2)], axis=1),
            jnp.concatenate([jnp.where(low_half, far[r], tile[r + 1]) for r in (0, 2)], axis=1),
        ]
    out = right_dot(*split(jnp.concatenate(rows, axis=0)), kz_ref[...])
    for j in range(BOX):
        x = out[BOX * (j // 2) : BOX * (j // 2 + 1), 256 * (j % 2) : 256 * (j % 2 + 1)]
        re, im = left_dot(ker_ref[...], x, 1)
        out_ref[0, j] = re
        out_ref[1, j] = im


def get(ref, *index):
    return ref[(0,) + index], ref[(1,) + index]


def put(ref, value, *index):
    ref[(0,) + index] = value[0]
    ref[(1,) + index] = value[1]


def body(
    own_ref, before_ref, after_ref, kern_a, kern_b,
    mask_re, mask_im, tz_ref, fwd_ref, inv_ref, inv_m_ref, bz_two, bz_hi, bm_ref, copies_ref,
    top_ref, next_ref,
    spec, kspec, fspec, work, slab, back, back_m, plain, u_hi, u_lo,
):
    filled = float(sphere_np().sum())
    lane = lax.broadcasted_iota(jnp.int32, (1, LANES), 1)
    odd_quarter = lane % GRID >= BOX

    def tile(step):
        return pl.ds(pl.multiple_of(step * 8, 8), 8)

    def kernels_first(at, n2, slot):
        for g, kern in enumerate((kern_a, kern_b)):
            x = eight_of_four([get(kern, n2 + 8 * m, at) for m in range(4)], 1)
            for k1 in range(8):
                put(work.at[2 * slot + g], twiddle(x[k1], n2 * k1, GRID), k1, n2)

    def kernels_second(at, k1, slot):
        for g in range(2):
            x = eight([get(work.at[2 * slot + g], k1, n2) for n2 in range(8)], 1)
            for k2 in range(8):
                put(kspec.at[g], x[k2], k1 + 8 * k2, at)

    low_half = lane < GRID
    row_odd = lax.broadcasted_iota(jnp.int32, (GRID, 2 * LANES), 0) % 2 == 1
    col_upper = lax.broadcasted_iota(jnp.int32, (GRID, 2 * LANES), 1) % LANES >= GRID
    parity = jnp.where(jnp.logical_and(row_odd, col_upper), -1.0, 1.0).astype(F32)
    def along_z(step):
        ref, start = ((before_ref, 0), (own_ref, 2), (after_ref, 6))[(step >= 2) + (step >= 6)]
        one = ref[8 * (step - start) : 8 * (step - start) + 8].reshape(8 * BOX, LANES)
        two = one * one
        lower = jnp.where(low_half, one, pltpu.roll(two, GRID, 1))
        upper = jnp.where(low_half, pltpu.roll(one, GRID, 1), two)
        rows = [v[BOX * e : BOX * (e + 1)] for e in range(8) for v in (lower, upper)]
        hi, lo = split(jnp.concatenate(rows, axis=0))
        slab[step % 2] = right_dot(hi, lo, tz_ref[...])

    along_z(0)
    for step in range(8):
        at = slice(8 * step, 8 * step + 8)
        if step < 7:
            along_z(step + 1)
        for e in range(8):
            kernels_first(at, e, step % 2)
        for e in range(8):
            re, im = left_dot(fwd_ref[...], slab[step % 2, GRID * e : GRID * (e + 1)] * parity, -1)
            spec[0, 8 * step + e] = re
            spec[1, 8 * step + e] = im
            kernels_second(at, e, step % 2)

    def finish(place, at, slot):
        for n2 in range(8):
            x = eight([get(work.at[slot], n2, k1) for k1 in range(8)], 1, keep=4)
            for n1 in range(4):
                put(place, x[n1], n2 + 8 * n1, at)

    @pl.loop(0, 4)
    def _(step):
        at = tile(step)
        for n2 in range(8):
            x = eight([get(spec, n2 + 8 * m, at) for m in range(8)], -1)
            for k1 in range(8):
                put(work.at[0], twiddle(x[k1], -n2 * k1, GRID), k1, n2)
        for k1 in range(8):
            x = eight([get(work.at[0], k1, n2) for n2 in range(8)], -1)
            prod = []
            for k2 in range(8):
                k = k1 + 8 * k2
                re, im = x[k2]
                put(plain, (re, im), k)
                a, b = mask_re[k, at], mask_im[k, at]
                prod.append((re * a - im * b, re * b + im * a))
            prod = eight(prod, 1)
            for n2 in range(8):
                put(work.at[1], twiddle(prod[n2], k1 * n2, GRID), n2, k1)
        for c in range(2):
            out = dot(jnp.concatenate(split(plain[c].reshape(GRID * 8, LANES)), axis=1), copies_ref[...])
            fspec[c, :, at] = out[:, :LANES].reshape(GRID, 8, LANES)
            fspec[c, :, tile(step + 4)] = out[:, LANES:].reshape(GRID, 8, LANES)
        finish(back_m, at, 1)

    def product_along_y(at, g, k1):
        prod = []
        for k2 in range(8):
            k = k1 + 8 * k2
            a, b = get(fspec, k, at)
            re, im = get(kspec.at[g], k, at)
            prod.append((re * a - im * b, re * b + im * a))
        prod = eight(prod, 1)
        for n2 in range(8):
            put(work.at[g], twiddle(prod[n2], k1 * n2, GRID), n2, k1)

    def along_x(y, s):
        if s == 2:
            hi, lo = split(jnp.concatenate([back_m[0, y], back_m[1, y]], axis=1))
            out = dot(inv_m_ref[...], jnp.concatenate([hi, lo, hi], axis=0))
            first, other = joined_parts(out[: 2 * BOX], 1), joined_parts(out[2 * BOX :], 1)
            res = [jnp.where(low_half, a, b) for a, b in zip(first, other)]
        else:
            res = left_dot(inv_ref[...], jnp.concatenate([back[s, 0, y], back[s, 1, y]], axis=1), 1)
        hi, lo = split(jnp.concatenate(res, axis=1))
        rows = pl.ds(pl.multiple_of(y * BOX, BOX), BOX)
        u_hi[s, rows, :] = hi
        u_lo[s, rows, :] = lo

    for g, s in ((0, 2), (1, 0)):

        @pl.loop(0, 8, unroll=4)
        def _(step, g=g, s=s):
            at = tile(step)
            for k1 in range(8):
                product_along_y(at, g, k1)
                if k1 % 2:
                    along_x(4 * step + k1 // 2, s)
            finish(back.at[g], at, g)

    for y in range(BOX):
        along_x(y, 1)

    def merged(one, other):
        return jnp.maximum(one[0], other[0]), jnp.maximum(jnp.minimum(one[0], other[0]), jnp.maximum(one[1], other[1]))

    quarter = lane // BOX
    for part in range(2):
        rows = pl.ds(512 * part, 512)
        sums = right_dot(u_hi[2, rows, :], u_lo[2, rows, :], bm_ref[...])
        mean = sums[:, :LANES] / filled
        var = jnp.maximum(sums[:, LANES:] / filled - mean * mean, 0.0)
        scale = 1.0 / (np.float32(np.sqrt(filled)) * jnp.sqrt(var + EPSILON))
        corr = []
        for g in range(2):
            both = dot(u_hi[g, rows, :], bz_two[...])
            corr.append((both[:, :LANES] + both[:, LANES:] + dot(u_lo[g, rows, :], bz_hi[...])) * scale)
        best = jnp.maximum(corr[0], corr[1]), jnp.minimum(corr[0], corr[1])
        best = merged(best, [pltpu.roll(v, GRID, 1) for v in best])
        best = merged(best, [pltpu.roll(v, BOX, 1) for v in best])
        for ref, v in zip((top_ref, next_ref), best):
            for e in range(4):
                y = [v[BOX * (4 * e + q) : BOX * (4 * e + q + 1)] for q in range(4)]
                o = jnp.where(quarter < 2, jnp.where(quarter == 0, y[0], y[1]), jnp.where(quarter == 2, y[2], y[3]))
                ref[:, LANES * (4 * part + e) : LANES * (4 * part + e + 1)] = o


def shifts(count, step):
    return [(i, i + step) for i in range(count) if 0 <= i + step < count]


def local(tomogram, templates):
    tx, ty, rots = lax.axis_size("tx"), lax.axis_size("ty"), lax.axis_size("rot")
    tile = jnp.swapaxes(tomogram, 0, 1)

    def pack(part):
        return jnp.concatenate([part[:HALF], part[HALF:]], axis=2)

    def unpack(part):
        return jnp.concatenate([part[:, :, :GRID], part[:, :, GRID:]], axis=0)

    up, down, templates = lax.optimization_barrier((pack(tile[:, HALF:]), pack(tile[:, :HALF]), templates))
    before = lax.ppermute(up, "tx", shifts(tx, 1))
    after = lax.ppermute(down, "tx", shifts(tx, -1))

    core = lax.rem(lax.axis_index("ty"), 2)
    mine = lax.dynamic_slice_in_dim(templates, core, 1, axis=0)
    far = [lax.ppermute(mine, "rot", [(i, (i + s) % rots) for i in range(rots)]) for s in range(1, rots)]
    far = jnp.concatenate(far, axis=0)
    core_far = lax.ppermute(far, "ty", [(i, i + 1 - 2 * (i % 2)) for i in range(ty)])

    grid = jnp.concatenate(
        [
            jnp.concatenate([unpack(before), tile[:, :HALF]], axis=1),
            jnp.concatenate([tile[:, HALF:], unpack(after)], axis=1),
        ],
        axis=2,
    )
    low = lax.ppermute(grid[HALF:], "ty", shifts(ty, 1))
    high = lax.ppermute(grid[:HALF], "ty", shifts(ty, -1))
    first = prep_call(templates[0], templates[1], far[0], far[1])
    second = prep_call(far[2], core_far[0], core_far[1], core_far[2])
    return kernel_call(grid, low, high, first, second)


def prep_call(*four_templates):
    mask, _, _, _, kz, _, ker = tables()[:7]
    return pl.pallas_call(
        prep,
        out_shape=jax.ShapeDtypeStruct((2, BOX, GRID, LANES), F32),
        compiler_params=pltpu.CompilerParams(vmem_limit_bytes=16 * 1024 * 1024),
        cost_estimate=pl.CostEstimate(flops=2 * 10**9, bytes_accessed=4 * 10**6, transcendentals=0),
        name="prep",
    )(*four_templates, *[jnp.asarray(t) for t in (mask, kz, ker)])


def kernel_call(grid, low, high, first, second):
    out = jax.ShapeDtypeStruct((BOX, BOX * BOX), F32)
    scratch = [
        pltpu.VMEM((2, GRID, BOX, LANES), F32),
        pltpu.VMEM((2, 2, GRID, GRID, LANES), F32),
        pltpu.VMEM((2, GRID, GRID, LANES), F32),
        pltpu.VMEM((4, 2, 8, 8, 8, LANES), F32),
        pltpu.VMEM((2, 8 * GRID, 2 * LANES), F32),
        pltpu.VMEM((2, 2, BOX, GRID, LANES), F32),
        pltpu.VMEM((2, BOX, BOX, LANES), F32),
        pltpu.VMEM((2, GRID, 8, LANES), F32),
        pltpu.VMEM((3, BOX * BOX, 2 * LANES), BF16),
        pltpu.VMEM((3, BOX * BOX, 2 * LANES), BF16),
    ]
    _, mask_re, mask_im, tz, _, fwd, _, inv, inv_m, *back = tables()
    return pl.pallas_call(
        body,
        out_shape=(out, out),
        scratch_shapes=scratch,
        compiler_params=pltpu.CompilerParams(vmem_limit_bytes=40 * 1024 * 1024),
        cost_estimate=pl.CostEstimate(flops=10**10, bytes_accessed=10**7, transcendentals=0),
        name="scores",
    )(grid, low, high, first, second, *[jnp.asarray(t) for t in (mask_re, mask_im, tz, fwd, inv, inv_m, *back)])


def solution(mesh):
    placed = (P("tx", "ty", None), P("rot", None, None))
    return jax.shard_map(
        local, mesh=mesh, in_specs=placed, out_specs=(P("tx", "ty"), P("tx", "ty")), check_vma=False
    )
```

```python
import functools
import math

import jax
import jax.numpy as jnp
import ml_dtypes
import numpy as np
from jax import lax
from jax.experimental import pallas as pl
from jax.experimental.pallas import tpu as pltpu
from jax.sharding import PartitionSpec as P

RADIUS = 15
EPSILON = 1e-05
GRID = 64
BOX = 32
HALF = 16
LANES = 128
F32 = jnp.float32
BF16 = jnp.bfloat16


def halves(table):
    hi = table.astype(ml_dtypes.bfloat16)
    lo = (table - hi.astype(np.float64)).astype(ml_dtypes.bfloat16)
    return hi, lo


def stacked(table):
    hi, lo = halves(table)
    return np.concatenate([hi, hi, lo], axis=0)


def wave(out_pos, in_pos):
    angle = 2.0 * np.pi / GRID * np.outer(out_pos, in_pos)
    return np.cos(angle), np.sin(angle)


def left_table(out_pos, in_pos, scale):
    cos, sin = wave(out_pos, in_pos)
    hi, lo = halves(np.concatenate([cos, sin], axis=0) * scale)
    return np.concatenate([hi, hi, lo], axis=1)


def sphere_np():
    centred = np.arange(BOX) - (BOX - 1) / 2.0
    sq = centred[:, None, None] ** 2 + centred[None, :, None] ** 2 + centred[None, None, :] ** 2
    return (sq <= float(RADIUS * RADIUS)).astype(np.float64)


def block(rows, cols, parts):
    some = next(iter(parts.values()))
    full = np.zeros((rows, cols) + some.shape)
    for at, part in parts.items():
        full[at] = part
    return full.transpose(0, 2, 1, 3).reshape(rows * some.shape[0], cols * some.shape[1])


@functools.cache
def tables():
    freq = np.arange(GRID)
    odd = np.arange(BOX) + 0.5
    centre = (BOX - 1) / 2.0
    cz, sz = wave(np.arange(GRID), odd)
    tomo = {}
    for kind in range(2):
        for dup in range(2):
            tomo[kind, 2 * dup + kind] = cz
            tomo[kind, 4 + 2 * dup + kind] = -sz
    tomo_hi, tomo_lo = halves(block(2, 8, tomo))
    ct, st = wave(np.arange(BOX), odd)
    kern = {}
    for rot in range(4):
        for jj in range(2):
            kern[2 * rot + jj, 8 * jj + rot] = ct
            kern[2 * rot + jj, 8 * jj + 4 + rot] = st
    kern_z = block(8, 16, kern)
    ci, si = wave(odd, np.arange(BOX))
    cm, sm = wave(odd, np.arange(BOX) + centre)
    back, back_mask = {}, {}
    for vol in range(4):
        back[vol, vol] = ci / BOX
        back[4 + vol, vol] = -si / BOX
    for row in range(4):
        for copy in range(4):
            back_mask[row, 4 * (row % 2) + copy] = cm / BOX
            back_mask[4 + row, 4 * (row % 2) + copy] = -sm / BOX
    back_hi, back_lo = halves(block(8, 4, back))
    back_mask_z = block(8, 8, back_mask)
    one = np.eye(BOX)
    copies = block(8, 8, {(row, col): one for half in (0, 4) for row, first in ((half, 0), (half + 2, 4)) for col in range(first, first + 4)})
    sphere = sphere_np()
    shifted = np.arange(BOX) - centre
    cx, sx = wave(freq, shifted)
    cy, sy = wave(freq, np.arange(BOX))
    co, so = wave(odd, shifted)
    spec = np.einsum("ai,bj,ck,ijk->bac", cx + 1j * sx, cy + 1j * sy, co + 1j * so, sphere, optimize=True)
    spec = np.concatenate([spec[:, :BOX], spec[:, :BOX], spec[:, BOX:], spec[:, BOX:]], axis=2)
    mask_re, mask_im = spec.real.astype(np.float32), spec.imag.astype(np.float32)
    mask = sphere.reshape(BOX, BOX * BOX).astype(np.float32)
    scale = 1.0 / (GRID * GRID)
    return (
        mask,
        mask_re,
        mask_im,
        np.concatenate([tomo_hi, tomo_hi, tomo_lo], axis=0),
        stacked(kern_z),
        left_table(freq[:BOX], np.arange(GRID), 1.0),
        left_table(freq, np.arange(BOX), 1.0),
        left_table(np.arange(BOX), freq, scale),
        np.concatenate([left_table(np.arange(BOX) + centre, f, scale) for f in (freq[:BOX], freq[BOX:])], axis=0),
        np.concatenate([back_hi, back_lo], axis=1),
        back_hi,
        stacked(back_mask_z),
        copies.astype(ml_dtypes.bfloat16),
    )


def split(x):
    hi = x.astype(BF16)
    return hi, (x - hi.astype(F32)).astype(BF16)


def dot(a, b):
    return jnp.dot(a, b, preferred_element_type=F32)


def right_dot(hi, lo, table):
    return dot(jnp.concatenate([hi, lo, hi], axis=1), table)


def left_dot(table, x, sign):
    hi, lo = split(x)
    return joined_parts(dot(table, jnp.concatenate([hi, lo, hi], axis=0)), sign)


def joined_parts(out, sign):
    n = out.shape[0] // 2
    tr, ti, br, bi = out[:n, :LANES], out[:n, LANES:], out[n:, :LANES], out[n:, LANES:]
    if sign > 0:
        return tr - bi, ti + br
    return tr + bi, ti - br


def add(a, b):
    return a[0] + b[0], a[1] + b[1]


def sub(a, b):
    return a[0] - b[0], a[1] - b[1]


def turn(a, sign):
    return (-a[1], a[0]) if sign > 0 else (a[1], -a[0])


def add_turned(a, b, sign):
    return (a[0] - b[1], a[1] + b[0]) if sign > 0 else (a[0] + b[1], a[1] - b[0])


def twiddle(a, num, den):
    num = num % den
    if num == 0:
        return a
    c, s = math.cos(2 * math.pi * num / den), math.sin(2 * math.pi * num / den)
    if 4 * num % den == 0:
        quarter = 4 * num // den
        return [a, turn(a, 1), (-a[0], -a[1]), turn(a, -1)][quarter]
    if 8 * num % den == 0:
        h = math.sqrt(0.5)
        odd = 8 * num // den
        if odd == 1:
            return (a[0] - a[1]) * h, (a[0] + a[1]) * h
        if odd == 3:
            return (a[0] + a[1]) * -h, (a[0] - a[1]) * h
        if odd == 5:
            return (a[1] - a[0]) * h, (a[0] + a[1]) * -h
        return (a[0] + a[1]) * h, (a[1] - a[0]) * h
    return a[0] * c - a[1] * s, a[0] * s + a[1] * c


def four(x, sign):
    a, b, c, d = add(x[0], x[2]), sub(x[0], x[2]), add(x[1], x[3]), sub(x[1], x[3])
    return [add(a, c), add_turned(b, d, sign), sub(a, c), add_turned(b, d, -sign)]


def eight(x, sign, keep=8):
    even, odd = four(x[0::2], sign), four(x[1::2], sign)
    odd = [odd[0], twiddle(odd[1], sign, 8), odd[2], twiddle(odd[3], 3 * sign, 8)]
    low = [add(even[0], odd[0]), add(even[1], odd[1]), add_turned(even[2], odd[2], sign), add(even[3], odd[3])]
    if keep == 4:
        return low
    return low + [sub(even[0], odd[0]), sub(even[1], odd[1]), add_turned(even[2], odd[2], -sign), sub(even[3], odd[3])]


def eight_of_four(x, sign):
    even = four(x, sign)
    odd = four([twiddle(x[m], sign * m, 8) for m in range(4)], sign)
    return [part for pair in zip(even, odd) for part in pair]


def prep(*refs):
    rotations, (mask_ref, kz_ref, ker_ref, out_ref) = refs[:4], refs[4:]
    filled = float(sphere_np().sum())
    low_half = lax.broadcasted_iota(jnp.int32, (1, LANES), 1) < GRID
    mask = mask_ref[...]
    normed = []
    for ref in rotations:
        t = ref[...]
        mu = jnp.sum(jnp.sum(t * mask, axis=0, keepdims=True), axis=1, keepdims=True) / filled
        d = (t - mu) * mask
        v = jnp.sum(jnp.sum(d * d, axis=0, keepdims=True), axis=1, keepdims=True) / filled
        normed.append(d * (1.0 / jnp.sqrt(v + EPSILON)))
    rows = []
    for jg in range(8):
        tile = [t[:, LANES * jg : LANES * (jg + 1)] for t in normed]
        far = [pltpu.roll(t, GRID, 1) for t in tile]
        rows += [
            jnp.concatenate([jnp.where(low_half, tile[r], far[r + 1]) for r in (0, 2)], axis=1),
            jnp.concatenate([jnp.where(low_half, far[r], tile[r + 1]) for r in (0, 2)], axis=1),
        ]
    out = right_dot(*split(jnp.concatenate(rows, axis=0)), kz_ref[...])
    for j in range(BOX):
        x = out[BOX * (j // 2) : BOX * (j // 2 + 1), 256 * (j % 2) : 256 * (j % 2 + 1)]
        re, im = left_dot(ker_ref[...], x, 1)
        out_ref[0, j] = re
        out_ref[1, j] = im


def get(ref, *index):
    return ref[(0,) + index], ref[(1,) + index]


def put(ref, value, *index):
    ref[(0,) + index] = value[0]
    ref[(1,) + index] = value[1]


def body(
    own_ref, before_ref, after_ref, kern_a, kern_b,
    mask_re, mask_im, tz_ref, fwd_ref, inv_ref, inv_m_ref, bz_two, bz_hi, bm_ref, copies_ref,
    top_ref, next_ref,
    spec, kspec, fspec, work, slab, back, back_m, plain, u_hi, u_lo, scales,
):
    filled = float(sphere_np().sum())
    lane = lax.broadcasted_iota(jnp.int32, (1, LANES), 1)
    odd_quarter = lane % GRID >= BOX

    def tile(step):
        return pl.ds(pl.multiple_of(step * 8, 8), 8)

    def kernels_first(at, n2, slot):
        for g, kern in enumerate((kern_a, kern_b)):
            x = eight_of_four([get(kern, n2 + 8 * m, at) for m in range(4)], 1)
            for k1 in range(8):
                put(work.at[2 * slot + g], twiddle(x[k1], n2 * k1, GRID), k1, n2)

    def kernels_second(at, k1, slot):
        for g in range(2):
            x = eight([get(work.at[2 * slot + g], k1, n2) for n2 in range(8)], 1)
            for k2 in range(8):
                put(kspec.at[g], x[k2], k1 + 8 * k2, at)

    low_half = lane < GRID
    row_odd = lax.broadcasted_iota(jnp.int32, (GRID, 2 * LANES), 0) % 2 == 1
    col_upper = lax.broadcasted_iota(jnp.int32, (GRID, 2 * LANES), 1) % LANES >= GRID
    parity = jnp.where(jnp.logical_and(row_odd, col_upper), -1.0, 1.0).astype(F32)
    def along_z(step):
        ref, start = ((before_ref, 0), (own_ref, 2), (after_ref, 6))[(step >= 2) + (step >= 6)]
        one = ref[8 * (step - start) : 8 * (step - start) + 8].reshape(8 * BOX, LANES)
        two = one * one
        lower = jnp.where(low_half, one, pltpu.roll(two, GRID, 1))
        upper = jnp.where(low_half, pltpu.roll(one, GRID, 1), two)
        rows = [v[BOX * e : BOX * (e + 1)] for e in range(8) for v in (lower, upper)]
        hi, lo = split(jnp.concatenate(rows, axis=0))
        slab[step % 2] = right_dot(hi, lo, tz_ref[...])

    along_z(0)
    for step in range(8):
        at = slice(8 * step, 8 * step + 8)
        if step < 7:
            along_z(step + 1)
        for e in range(8):
            kernels_first(at, e, step % 2)
        for e in range(8):
            re, im = left_dot(fwd_ref[...], slab[step % 2, GRID * e : GRID * (e + 1)] * parity, -1)
            spec[0, 8 * step + e] = re
            spec[1, 8 * step + e] = im
            kernels_second(at, e, step % 2)

    def finish(place, at, slot):
        for n2 in range(8):
            x = eight([get(work.at[slot], n2, k1) for k1 in range(8)], 1, keep=4)
            for n1 in range(4):
                put(place, x[n1], n2 + 8 * n1, at)

    @pl.loop(0, 4)
    def _(step):
        at = tile(step)
        for n2 in range(8):
            x = eight([get(spec, n2 + 8 * m, at) for m in range(8)], -1)
            for k1 in range(8):
                put(work.at[0], twiddle(x[k1], -n2 * k1, GRID), k1, n2)
        for k1 in range(8):
            x = eight([get(work.at[0], k1, n2) for n2 in range(8)], -1)
            prod = []
            for k2 in range(8):
                k = k1 + 8 * k2
                re, im = x[k2]
                put(plain, (re, im), k)
                a, b = mask_re[k, at], mask_im[k, at]
                prod.append((re * a - im * b, re * b + im * a))
            prod = eight(prod, 1)
            for n2 in range(8):
                put(work.at[1], twiddle(prod[n2], k1 * n2, GRID), n2, k1)
        for c in range(2):
            out = dot(jnp.concatenate(split(plain[c].reshape(GRID * 8, LANES)), axis=1), copies_ref[...])
            fspec[c, :, at] = out[:, :LANES].reshape(GRID, 8, LANES)
            fspec[c, :, tile(step + 4)] = out[:, LANES:].reshape(GRID, 8, LANES)
        finish(back_m, at, 1)

    def product_along_y(at, g, k1):
        prod = []
        for k2 in range(8):
            k = k1 + 8 * k2
            a, b = get(fspec, k, at)
            re, im = get(kspec.at[g], k, at)
            prod.append((re * a - im * b, re * b + im * a))
        prod = eight(prod, 1)
        for n2 in range(8):
            put(work.at[g], twiddle(prod[n2], k1 * n2, GRID), n2, k1)

    def along_x(y, s):
        if s == 2:
            hi, lo = split(jnp.concatenate([back_m[0, y], back_m[1, y]], axis=1))
            out = dot(inv_m_ref[...], jnp.concatenate([hi, lo, hi], axis=0))
            first, other = joined_parts(out[: 2 * BOX], 1), joined_parts(out[2 * BOX :], 1)
            res = [jnp.where(low_half, a, b) for a, b in zip(first, other)]
        else:
            res = left_dot(inv_ref[...], jnp.concatenate([back[s, 0, y], back[s, 1, y]], axis=1), 1)
        hi, lo = split(jnp.concatenate(res, axis=1))
        rows = pl.ds(pl.multiple_of(y * BOX, BOX), BOX)
        u_hi[s, rows, :] = hi
        u_lo[s, rows, :] = lo

    def divisors(step):
        rows = pl.ds(pl.multiple_of(step * LANES, LANES), LANES)
        sums = right_dot(u_hi[2, rows, :], u_lo[2, rows, :], bm_ref[...])
        mean = sums[:, :LANES] / filled
        var = jnp.maximum(sums[:, LANES:] / filled - mean * mean, 0.0)
        scales[rows, :] = 1.0 / (np.float32(np.sqrt(filled)) * jnp.sqrt(var + EPSILON))

    for g, s in ((0, 2), (1, 0)):

        @pl.loop(0, 8, unroll=4)
        def _(step, g=g, s=s):
            at = tile(step)
            for k1 in range(8):
                product_along_y(at, g, k1)
                if k1 % 2:
                    along_x(4 * step + k1 // 2, s)
            if g == 1:
                divisors(step)
            finish(back.at[g], at, g)

    for y in range(BOX):
        along_x(y, 1)

    def merged(one, other):
        return jnp.maximum(one[0], other[0]), jnp.maximum(jnp.minimum(one[0], other[0]), jnp.maximum(one[1], other[1]))

    quarter = lane // BOX
    for part in range(2):
        rows = pl.ds(512 * part, 512)
        scale = scales[rows, :]
        corr = []
        for g in range(2):
            both = dot(u_hi[g, rows, :], bz_two[...])
            corr.append((both[:, :LANES] + both[:, LANES:] + dot(u_lo[g, rows, :], bz_hi[...])) * scale)
        best = jnp.maximum(corr[0], corr[1]), jnp.minimum(corr[0], corr[1])
        best = merged(best, [pltpu.roll(v, GRID, 1) for v in best])
        best = merged(best, [pltpu.roll(v, BOX, 1) for v in best])
        for ref, v in zip((top_ref, next_ref), best):
            for e in range(4):
                y = [v[BOX * (4 * e + q) : BOX * (4 * e + q + 1)] for q in range(4)]
                o = jnp.where(quarter < 2, jnp.where(quarter == 0, y[0], y[1]), jnp.where(quarter == 2, y[2], y[3]))
                ref[:, LANES * (4 * part + e) : LANES * (4 * part + e + 1)] = o


def shifts(count, step):
    return [(i, i + step) for i in range(count) if 0 <= i + step < count]


def local(tomogram, templates):
    tx, ty, rots = lax.axis_size("tx"), lax.axis_size("ty"), lax.axis_size("rot")
    tile = jnp.swapaxes(tomogram, 0, 1)

    def pack(part):
        return jnp.concatenate([part[:HALF], part[HALF:]], axis=2)

    def unpack(part):
        return jnp.concatenate([part[:, :, :GRID], part[:, :, GRID:]], axis=0)

    up, down, templates = lax.optimization_barrier((pack(tile[:, HALF:]), pack(tile[:, :HALF]), templates))
    before = lax.ppermute(up, "tx", shifts(tx, 1))
    after = lax.ppermute(down, "tx", shifts(tx, -1))

    core = lax.rem(lax.axis_index("ty"), 2)
    mine = lax.dynamic_slice_in_dim(templates, core, 1, axis=0)
    far = [lax.ppermute(mine, "rot", [(i, (i + s) % rots) for i in range(rots)]) for s in range(1, rots)]
    far = jnp.concatenate(far, axis=0)
    core_far = lax.ppermute(far, "ty", [(i, i + 1 - 2 * (i % 2)) for i in range(ty)])

    grid = jnp.concatenate(
        [
            jnp.concatenate([unpack(before), tile[:, :HALF]], axis=1),
            jnp.concatenate([tile[:, HALF:], unpack(after)], axis=1),
        ],
        axis=2,
    )
    low = lax.ppermute(grid[HALF:], "ty", shifts(ty, 1))
    high = lax.ppermute(grid[:HALF], "ty", shifts(ty, -1))
    first = prep_call(templates[0], templates[1], far[0], far[1])
    second = prep_call(far[2], core_far[0], core_far[1], core_far[2])
    return kernel_call(grid, low, high, first, second)


def prep_call(*four_templates):
    mask, _, _, _, kz, _, ker = tables()[:7]
    return pl.pallas_call(
        prep,
        out_shape=jax.ShapeDtypeStruct((2, BOX, GRID, LANES), F32),
        compiler_params=pltpu.CompilerParams(vmem_limit_bytes=16 * 1024 * 1024),
        cost_estimate=pl.CostEstimate(flops=2 * 10**9, bytes_accessed=4 * 10**6, transcendentals=0),
        name="prep",
    )(*four_templates, *[jnp.asarray(t) for t in (mask, kz, ker)])


def kernel_call(grid, low, high, first, second):
    out = jax.ShapeDtypeStruct((BOX, BOX * BOX), F32)
    scratch = [
        pltpu.VMEM((2, GRID, BOX, LANES), F32),
        pltpu.VMEM((2, 2, GRID, GRID, LANES), F32),
        pltpu.VMEM((2, GRID, GRID, LANES), F32),
        pltpu.VMEM((4, 2, 8, 8, 8, LANES), F32),
        pltpu.VMEM((2, 8 * GRID, 2 * LANES), F32),
        pltpu.VMEM((2, 2, BOX, GRID, LANES), F32),
        pltpu.VMEM((2, BOX, BOX, LANES), F32),
        pltpu.VMEM((2, GRID, 8, LANES), F32),
        pltpu.VMEM((3, BOX * BOX, 2 * LANES), BF16),
        pltpu.VMEM((3, BOX * BOX, 2 * LANES), BF16),
        pltpu.VMEM((BOX * BOX, LANES), F32),
    ]
    _, mask_re, mask_im, tz, _, fwd, _, inv, inv_m, *back = tables()
    return pl.pallas_call(
        body,
        out_shape=(out, out),
        scratch_shapes=scratch,
        compiler_params=pltpu.CompilerParams(vmem_limit_bytes=40 * 1024 * 1024),
        cost_estimate=pl.CostEstimate(flops=10**10, bytes_accessed=10**7, transcendentals=0),
        name="scores",
    )(grid, low, high, first, second, *[jnp.asarray(t) for t in (mask_re, mask_im, tz, fwd, inv, inv_m, *back)])


def solution(mesh):
    placed = (P("tx", "ty", None), P("rot", None, None))
    return jax.shard_map(
        local, mesh=mesh, in_specs=placed, out_specs=(P("tx", "ty"), P("tx", "ty")), check_vma=False
    )
```
